32 devices in a mesh: sess: 8 (over z, core), tp: 4 (over y, x).
Axes of the slice: x: 2, y: 2, z: 4, core: 2. Of those that a mesh axis runs over, the one named last changes fastest.
Arguments:
- frames: bfloat16 [128, 4096], P('sess', 'tp'), may hold values from -6 to 6
- norm_gain: bfloat16 [4096], replicated, may hold values from 0.5 to 1.5
- w_qkv: bfloat16 [3, 4096, 2048], P(None, None, 'tp'), may hold values from -0.09375 to 0.09375
- w_out: bfloat16 [2048, 4096], P('tp'), may hold values from -0.5 to 0.5
- kv_cache: bfloat16 [2, 256, 375, 2048], P(None, 'sess', None, 'tp'), may hold values from -800 to 800
- frame_session: int32 [128], replicated, may hold values from 0 to 127, as said below
- owner_of: int32 [128], replicated, may hold values from 0 to 7, as said below
- context_len: int32 [128], replicated, may hold values from 1 to 375, as said below
Outputs:
- hidden_rows: bfloat16 [128, 4096], P('sess', 'tp')
The draws below stay inside these ranges and needn't reach their ends.
Inputs may be any that keep to these rules, and one draw needn't show every extreme that they name: `frame_session`: a permutation of the sessions; at most 4 of the frame rows of one index of sess have the same owner, and some rows reach 4. `owner_of`: each owner holds at most 32 sessions, and some owner holds exactly 32. `context_len`: some session has exactly 375.
All inputs are finite; a program needn't handle non-finite values.
Results may differ from the reference program's by a relative error of at most 0.014.
The reference program's roundings to bfloat16 on the way (of `normed`, `projected`, `weights` and `attended`) count: a program that leaves them out, or rounds other values in their place, can miss the bound.
Values may be sent and summed in bfloat16 or wider, within the bound.
A program may use at most 128 MiB of HBM per device.

```python
import jax
import jax.numpy as jnp
from jax import lax

D = 4096
HEADS = 16
HD = 128
CTX = 375
SESS_DEV = 16
SESSIONS = 128
SLOTS = 32
N_SESS = 8


def session_layout(key):
    base_key = jax.random.fold_in(key, 7)
    key_heavy, key_offset, key_order = jax.random.split(base_key, 3)
    positions = jnp.arange(SESSIONS, dtype=jnp.int32)
    heavy = jax.random.randint(key_heavy, (), 0, N_SESS, dtype=jnp.int32)
    offset = jax.random.randint(key_offset, (), 0, N_SESS, dtype=jnp.int32)
    order = jax.random.permutation(key_order, SESSIONS).astype(jnp.int32)
    others = (positions - SLOTS) % (N_SESS - 1)
    owner_pos = jnp.where(positions < SLOTS, heavy, others + (others >= heavy).astype(jnp.int32))
    row_pos = (positions + offset) % N_SESS * SESS_DEV + positions // N_SESS
    frame_session = jnp.zeros((SESSIONS,), jnp.int32).at[row_pos].set(order)
    owner_of = jnp.zeros((SESSIONS,), jnp.int32).at[order].set(owner_pos.astype(jnp.int32))
    return (frame_session, owner_of)


def draw_frame_session(key, part):
    return session_layout(key)[0]


def draw_owner_of(key, part):
    return session_layout(key)[1]


def draw_context_len(key, part):
    lengths = jax.random.randint(jax.random.fold_in(key, 11), (SESSIONS,), 1, CTX + 1, dtype=jnp.int32)
    longest = jax.random.randint(jax.random.fold_in(key, 12), (), 0, SESSIONS, dtype=jnp.int32)
    return lengths.at[longest].set(CTX)


def draw_kv_cache(key, part):
    key_base = jax.random.fold_in(jax.random.fold_in(key, 13), 0)
    slot_total = N_SESS * SLOTS
    shape = (2, slot_total, CTX, HEADS * HD)
    scale = jnp.array([1.0, 2.0], jnp.float32)[:, None, None, None]
    whole = jnp.clip(jax.random.normal(key_base, shape, jnp.float32), -4.0, 4.0) * scale
    return whole.astype(jnp.bfloat16)


def block_scale(rng, extent, pieces, low, largest):
    def one(axis_at, shards_of):
        heights = jax.random.uniform(jax.random.fold_in(jax.random.fold_in(rng, 6), axis_at), (shards_of,), jnp.float32, low / len(pieces), largest / len(pieces))
        return jnp.repeat(jnp.exp(heights), extent[axis_at] // shards_of).reshape((-1,) + (1,) * (len(extent) - axis_at - 1))

    gain = one(*pieces[0])
    for cut in pieces[1:]:
        gain = gain * one(*cut)
    return gain


def scatter_about(own_key, shape, width, reach, cuts=(), held_as=jnp.bfloat16):
    gain = block_scale(own_key, shape, cuts, -0.22, 0.18) if cuts else 1.0
    values = jax.random.normal(own_key, shape, jnp.float32) * width * gain
    return jnp.minimum(jnp.maximum(values, -reach), reach).astype(held_as)


def setup_inputs(seed: int = 0) -> dict:
    key_of = jax.random.split(jax.random.key(seed), 9)
    return {
        "frames": scatter_about(key_of[0], (SESSIONS, D), 1.0, 6.0, ((0, 8), (1, 4))),
        "norm_gain": jnp.clip(1.0 + 0.1 * jax.random.normal(key_of[1], (D,), jnp.float32), 0.5, 1.5).astype(jnp.bfloat16),
        "w_qkv": scatter_about(key_of[2], (3, D, HEADS * HD), D ** -0.5, 0.09375, ((2, 4),)),
        "w_out": scatter_about(key_of[3], (HEADS * HD, D), HD ** -0.5, 0.5, ((0, 4),)),
        "kv_cache": draw_kv_cache(jax.random.fold_in(key_of[8], 71), 0),
        "frame_session": draw_frame_session(jax.random.fold_in(key_of[8], 71), 0),
        "owner_of": draw_owner_of(jax.random.fold_in(key_of[8], 71), 0),
        "context_len": draw_context_len(jax.random.fold_in(key_of[8], 71), 0),
    }


def attend_row(triple, cached, length):
    heads_count = triple.shape[1] // HD
    queries = triple[0].astype(jnp.float32).reshape(heads_count, HD)
    new_keys = triple[1].astype(jnp.float32).reshape(heads_count, HD)
    new_values = triple[2].astype(jnp.float32).reshape(heads_count, HD)
    cached_keys = cached[0].astype(jnp.float32).reshape(CTX, heads_count, HD)
    cached_values = cached[1].astype(jnp.float32).reshape(CTX, heads_count, HD)
    factor = 1.0 / jnp.sqrt(jnp.float32(HD))
    scores = jnp.einsum('hd,thd->ht', queries, cached_keys) * factor
    own_score = lax.optimization_barrier(jnp.sum(queries * new_keys, axis=-1)) * factor
    valid = jnp.arange(CTX, dtype=jnp.int32)[None, :] < length
    scores = jnp.where(valid, scores, -jnp.inf)
    top_score = jnp.maximum(lax.optimization_barrier(jnp.max(scores, axis=-1)), own_score)
    expo = jnp.where(valid, jnp.exp(scores - top_score[:, None]), 0.0)
    own_exp = jnp.exp(own_score - top_score)
    total = lax.optimization_barrier(jnp.sum(expo, axis=-1)) + own_exp
    weights = (expo / total[:, None]).astype(jnp.bfloat16).astype(jnp.float32)
    own_weight = (own_exp / total).astype(jnp.bfloat16).astype(jnp.float32)
    mixed = jnp.einsum('ht,thd->hd', weights, cached_values) + own_weight[:, None] * new_values
    return mixed.astype(jnp.bfloat16).reshape(heads_count * HD)

def reference(frames, norm_gain, w_qkv, w_out, kv_cache, frame_session, owner_of, context_len):
    wide = frames.astype(jnp.float32)
    normed = (wide * lax.rsqrt(lax.optimization_barrier(jnp.mean(wide * wide, axis=1, keepdims=True)) + 1e-05) * norm_gain.astype(jnp.float32)).astype(jnp.bfloat16)
    projected = jnp.einsum('rd,cde->rce', normed.astype(jnp.float32), w_qkv.astype(jnp.float32)).astype(jnp.bfloat16)
    session_ids = jnp.arange(SESSIONS, dtype=jnp.int32)
    same_owner = owner_of[:, None] == owner_of[None, :]
    slot_of = lax.optimization_barrier(jnp.sum(same_owner & (session_ids[None, :] < session_ids[:, None]), axis=1)).astype(jnp.int32)
    cache_row = (owner_of * SLOTS + slot_of)[frame_session].astype(jnp.int32)
    row_length = context_len[frame_session].astype(jnp.int32)

    def one_row(packed):
        triple, crow, length = packed
        cached = lax.dynamic_index_in_dim(kv_cache, crow, 1, keepdims=False)
        return attend_row(triple, cached, length)
    attended = lax.map(one_row, (projected, cache_row, row_length))
    branch = jnp.dot(attended, w_out, preferred_element_type=jnp.float32)
    return (wide + branch).astype(jnp.bfloat16)
```

```python
import functools

import jax
import jax.numpy as jnp
from jax import lax
from jax.experimental import pallas as pl
from jax.experimental.pallas import tpu as pltpu
from jax.sharding import PartitionSpec as P

HD = 128
LANES = 128
MESH = pl.DeviceIdType.MESH
F32 = jnp.float32
BF16 = jnp.bfloat16


def quot(x, k):
    if k & (k - 1) == 0:
        return lax.shift_right_logical(x, jnp.full_like(x, k.bit_length() - 1))
    return lax.div(x, jnp.full_like(x, k))


def rest(x, k):
    return x - quot(x, k) * k


def iota(rows, cols, axis):
    return lax.broadcasted_iota(jnp.int32, (rows, cols), axis)


def one_hot(cond):
    return jnp.where(cond, 1.0, 0.0).astype(BF16)


def routing(me, n, heads, cap, msg, rows, slots, sessions, fs, owner, length):
    def pick(cond, values, axis):
        return jnp.sum(jnp.where(cond, values, 0.0), axis=axis, keepdims=True)

    i0, i1 = iota(sessions, sessions, 0), iota(sessions, sessions, 1)
    eye = i0 == i1

    def as_col(row):
        return pick(eye, row, 1)

    owner_c = as_col(owner)
    slot_c = pick((owner_c == owner) & (i1 < i0), 1.0, 1)
    match = i0 == fs
    row_owner = pick(match, owner_c, 0)
    row_slot = pick(match, slot_c, 0)
    row_len = pick(match, as_col(length), 0)
    row_owner_c, row_slot_c = as_col(row_owner), as_col(row_slot)
    block0, block1 = quot(i0, rows), quot(i1, rows)
    row_pair = pick((row_owner_c == row_owner) & (block0 == block1) & (i0 < i1), 1.0, 0)
    target = row_owner * cap + row_pair
    place = quot(iota(1, sessions, 1), rows).astype(F32) * cap + row_pair
    target_c, place_c = as_col(target), as_col(place)
    me_f = me.astype(F32)

    stack, total, held = heads * rows, n * msg, heads * slots

    def message_code(i):
        inner = rest(i, msg)
        return quot(inner, cap), (quot(i, msg) * cap + rest(inner, cap)).astype(F32)

    local = pick(
        iota(sessions, stack, 0) == me * rows + rest(iota(sessions, stack, 1), rows), target_c, 0
    )
    head_i, code = message_code(iota(total, stack, 0))
    send = one_hot((head_i == quot(iota(total, stack, 1), rows)) & (code == local))
    local_c = pick(
        iota(stack, sessions, 1) == me * rows + rest(iota(stack, sessions, 0), rows), target, 1
    )
    head_i, code = message_code(iota(stack, total, 1))
    unsend = one_hot((head_i == quot(iota(stack, total, 0), rows)) & (code == local_c))

    in_slot = (row_slot == rest(iota(held, sessions, 0), slots).astype(F32)) & (row_owner == me_f)
    _, code = message_code(iota(sessions, total, 1))
    spread = jnp.dot(one_hot(in_slot), one_hot(place_c == code), preferred_element_type=F32)
    head_i, _ = message_code(iota(held, total, 1))
    collect = jnp.where(head_i == quot(iota(held, total, 0), slots), spread, 0.0).astype(BF16)
    in_slot_t = (row_slot_c == rest(iota(sessions, held, 1), slots).astype(F32)) & (
        row_owner_c == me_f
    )
    _, code = message_code(iota(total, sessions, 0))
    spread = jnp.dot(one_hot(place == code), one_hot(in_slot_t), preferred_element_type=F32)
    head_i, _ = message_code(iota(total, held, 0))
    uncollect = jnp.where(head_i == quot(iota(total, held, 1), slots), spread, 0.0).astype(BF16)

    held_len = pick(in_slot, row_len, 1)
    lane = iota(held, LANES, 1)
    limit = jnp.where(
        rest(lane, slots) == rest(iota(held, LANES, 0), slots),
        held_len - quot(lane, slots).astype(F32),
        -1.0,
    )
    return send, unsend, collect, uncollect, limit


def kernel(
    dims,
    frames_ref, gain_ref, fs_ref, owner_ref, length_ref, wqkv_hbm, wout_hbm, kv_hbm,
    out_ref,
    w_v, wo_v, kv_v, fr_all, normed, q_send, q_recv, kv_send, kv_recv, r_send, r_recv,
    p_send, p_recv, scores, acc, send_m, unsend_m, collect_m, uncollect_m, limit_m,
    load_sem, ag_s, ag_r, q_s, q_r, kv_s, kv_r, r_s, r_r, p_s, p_r,
):
    n, tp, heads, cap, msg, rows, slots, ctx, tchunk, chunks, kc = dims
    dl = frames_ref.shape[1]
    d_all = dl * tp
    me, mt = lax.axis_index("sess"), lax.axis_index("tp")
    sess_peer = [lax.rem(me + d, n) for d in range(n)]
    tp_peer = [lax.rem(mt + d, tp) for d in range(tp)]

    loads = []

    def load(src, dst):
        loads.append(pltpu.make_async_copy(src, dst, load_sem.at[len(loads)]))
        loads[-1].start()
        return loads[-1]

    w_load = [load(wqkv_hbm.at[c], w_v.at[c]) for c in range(3)]

    barrier = pltpu.get_barrier_semaphore()
    for d in range(1, tp):
        pl.semaphore_signal(barrier, inc=1, device_id=(me, tp_peer[d]), device_id_type=MESH)
    for d in range(1, n):
        pl.semaphore_signal(barrier, inc=1, device_id=(sess_peer[d], mt), device_id_type=MESH)
    pl.semaphore_wait(barrier, n + tp - 2)

    def over_tp(src, dst, s, r, d):
        copy = pltpu.make_async_remote_copy(
            src_ref=src, dst_ref=dst, send_sem=s.at[d - 1], recv_sem=r.at[d - 1],
            device_id=(me, tp_peer[d]), device_id_type=MESH,
        )
        copy.start()
        return copy

    def over_sess(send, recv, s, r):
        copies = []
        for d in range(1, n):
            copy = pltpu.make_async_remote_copy(
                src_ref=send.at[sess_peer[d]], dst_ref=recv.at[me],
                send_sem=s.at[d - 1], recv_sem=r.at[d - 1],
                device_id=(sess_peer[d], mt), device_id_type=MESH,
            )
            copy.start()
            copies.append(copy)
        return copies

    ag = [over_tp(frames_ref, fr_all.at[mt], ag_s, ag_r, d) for d in range(1, tp)]
    kv_load = []
    for c in range(2):
        parts = []
        for t0 in range(0, ctx, 4 * tchunk):
            size = min(4 * tchunk, ctx - t0)
            parts.append(
                load(kv_hbm.at[c, pl.ds(t0, size)], kv_v.at[c, pl.ds(t0, size)])
            )
        kv_load.append(parts)
    wo_load = load(wout_hbm, wo_v)

    pad = chunks * tchunk - ctx
    if pad:
        kv_v[:, ctx:] = jnp.zeros((2, pad) + kv_v.shape[2:], BF16)
    fr_all[mt] = frames_ref[...]
    send_m[...], unsend_m[...], collect_m[...], uncollect_m[...], limit_m[...] = routing(
        me, n, heads, cap, msg, rows, slots, fs_ref.shape[1],
        fs_ref[...], owner_ref[...].astype(F32), length_ref[...].astype(F32),
    )

    for copy in ag:
        copy.wait()
    square = jnp.zeros((rows, 1), F32)
    for b in range(tp):
        wide = fr_all[b].astype(F32)
        square += jnp.sum(wide * wide, axis=1, keepdims=True)
    scale = lax.rsqrt(square * (1.0 / d_all) + 1e-05)
    for b in range(tp):
        gain = gain_ref[:, b * dl : (b + 1) * dl].astype(F32)
        part = (fr_all[b].astype(F32) * scale * gain).astype(BF16)
        for k in range(dl // kc):
            normed[b * (dl // kc) + k] = part[:, k * kc : (k + 1) * kc]

    def project(c):
        w_load[c].wait()

        def step(k, total):
            block = w_v[c, pl.ds(pl.multiple_of(k * kc, kc), kc), :]
            return total + jnp.dot(normed[k], block, preferred_element_type=F32)

        out = lax.fori_loop(
            0, d_all // kc, step, jnp.zeros((rows, heads * HD), F32), unroll=2
        ).astype(BF16)
        stacked = jnp.concatenate([out[:, h * HD : (h + 1) * HD] for h in range(heads)], axis=0)
        placed = jnp.dot(send_m[...], stacked, preferred_element_type=F32)
        return placed.astype(BF16).reshape(n, msg, HD)

    q_send[...] = project(0)
    q_copies = over_sess(q_send, q_recv, q_s, q_r)
    q_recv[me] = q_send[me]
    kv_send[:, 0] = project(1)
    kv_send[:, 1] = project(2)
    kv_copies = over_sess(kv_send, kv_recv, kv_s, kv_r)
    kv_recv[me] = kv_send[me]

    def collected(block):
        return jnp.dot(
            collect_m[...], block.reshape(n * msg, HD), preferred_element_type=F32
        )

    factor = 1.0 / jnp.sqrt(jnp.float32(HD))
    held = heads * slots
    for copy in q_copies:
        copy.wait()
    query = collected(q_recv[...])
    head_row = quot(iota(held, HD, 0), slots)
    query_wide = jnp.concatenate(
        [jnp.where(head_row == h, query, 0.0) for h in range(heads)], axis=1
    ).astype(BF16)
    for copy in kv_load[0]:
        copy.wait()
    width = tchunk * slots
    tiles = width // LANES
    tile_t = LANES // slots
    limit = limit_m[...]

    def score_step(c, top):
        keys = kv_v[0, pl.ds(c * tchunk, tchunk)].reshape(width, heads * HD)
        s = lax.dot_general(
            query_wide, keys, (((1,), (1,)), ((), ())), preferred_element_type=F32
        )
        for k in range(tiles):
            edge = (c * tchunk + k * tile_t).astype(F32)
            tile = jnp.where(
                limit > edge, s[:, k * LANES : (k + 1) * LANES] * factor, -jnp.inf
            )
            scores[c, :, k * LANES : (k + 1) * LANES] = tile
            top = jnp.maximum(top, tile)
        return top

    top = lax.fori_loop(0, chunks, score_step, jnp.full((held, LANES), -jnp.inf, F32))

    for copy in kv_copies:
        copy.wait()
    new_key = collected(kv_recv[:, 0])
    new_value = collected(kv_recv[:, 1])
    own = jnp.sum(query * new_key, axis=1, keepdims=True) * factor
    top = jnp.maximum(jnp.max(top, axis=1, keepdims=True), own)
    top_wide = jnp.broadcast_to(top, (held, LANES))

    def exp_step(c, total):
        for k in range(tiles):
            e = jnp.exp(scores[c, :, k * LANES : (k + 1) * LANES] - top_wide)
            scores[c, :, k * LANES : (k + 1) * LANES] = e
            total = total + e
        return total

    total = lax.fori_loop(0, chunks, exp_step, jnp.zeros((held, LANES), F32))
    own_exp = jnp.exp(own - top)
    total = jnp.sum(total, axis=1, keepdims=True) + own_exp
    inverse = 1.0 / total
    own_weight = (own_exp * inverse).astype(BF16).astype(F32)

    for copy in kv_load[1]:
        copy.wait()
    acc[...] = jnp.zeros_like(acc)

    def mix_step(c, carry):
        weights = (scores[c] * inverse).astype(BF16)
        values = kv_v[1, pl.ds(c * tchunk, tchunk)].reshape(width, heads * HD)
        acc[...] += jnp.dot(weights, values, preferred_element_type=F32)
        return carry

    lax.fori_loop(0, chunks, mix_step, 0)
    mixed = jnp.concatenate(
        [acc[h * slots : (h + 1) * slots, h * HD : (h + 1) * HD] for h in range(heads)], axis=0
    )
    attended = (mixed + own_weight * new_value).astype(BF16)
    r_send[...] = (
        jnp.dot(uncollect_m[...], attended, preferred_element_type=F32)
        .astype(BF16)
        .reshape(n, msg, HD)
    )
    r_copies = over_sess(r_send, r_recv, r_s, r_r)
    r_recv[me] = r_send[me]
    wo_load.wait()
    for copy in r_copies:
        copy.wait()
    back = jnp.dot(
        unsend_m[...], r_recv[...].reshape(n * msg, HD), preferred_element_type=F32
    ).astype(BF16)
    mine = jnp.concatenate([back[h * rows : (h + 1) * rows] for h in range(heads)], axis=1)

    def branch(dest):
        block = wo_v[:, pl.ds(pl.multiple_of(dest * dl, dl), dl)]
        return jnp.dot(mine, block, preferred_element_type=F32)

    p_copies = []
    for d in range(1, tp):
        p_send[d - 1] = branch(tp_peer[d]).astype(BF16)
        p_copies.append(over_tp(p_send.at[d - 1], p_recv.at[d - 1], p_s, p_r, d))
    result = branch(mt)
    for d in range(1, tp):
        p_copies[d - 1].wait()
        result = result + p_recv[d - 1].astype(F32)
    out_ref[...] = (frames_ref[...].astype(F32) + result).astype(BF16)


def body(frames, norm_gain, w_qkv, w_out, kv_cache, frame_session, owner_of, context_len):
    n, tp = lax.axis_size("sess"), lax.axis_size("tp")
    rows, dl = frames.shape
    d_all, head_cols = w_qkv.shape[1:]
    slots, ctx = kv_cache.shape[1:3]
    sessions = frame_session.shape[0]
    heads = head_cols // HD
    cap = (slots + n - 1) // n
    msg = (heads * cap + 15) // 16 * 16
    tchunk = 1024 // slots
    chunks = (ctx + tchunk - 1) // tchunk
    kc = min(512, dl)
    held, total, stack = heads * slots, n * msg, heads * rows
    parts = (ctx + 4 * tchunk - 1) // (4 * tchunk)
    dims = (n, tp, heads, cap, msg, rows, slots, ctx, tchunk, chunks, kc)
    vmem = pl.BlockSpec(memory_space=pltpu.VMEM)
    hbm = pl.BlockSpec(memory_space=pl.ANY)
    dma = pltpu.SemaphoreType.DMA
    return pl.pallas_call(
        functools.partial(kernel, dims),
        out_shape=jax.ShapeDtypeStruct((rows, dl), BF16),
        in_specs=[vmem] * 5 + [hbm] * 3,
        out_specs=vmem,
        scratch_shapes=[
            pltpu.VMEM((3, d_all, head_cols), BF16),
            pltpu.VMEM((head_cols, d_all), BF16),
            pltpu.VMEM((2, chunks * tchunk, slots, head_cols), BF16),
            pltpu.VMEM((tp, rows, dl), BF16),
            pltpu.VMEM((d_all // kc, rows, kc), BF16),
            pltpu.VMEM((n, msg, HD), BF16),
            pltpu.VMEM((n, msg, HD), BF16),
            pltpu.VMEM((n, 2, msg, HD), BF16),
            pltpu.VMEM((n, 2, msg, HD), BF16),
            pltpu.VMEM((n, msg, HD), BF16),
            pltpu.VMEM((n, msg, HD), BF16),
            pltpu.VMEM((tp - 1, rows, dl), BF16),
            pltpu.VMEM((tp - 1, rows, dl), BF16),
            pltpu.VMEM((chunks, held, tchunk * slots), F32),
            pltpu.VMEM((held, head_cols), F32),
            pltpu.VMEM((total, stack), BF16),
            pltpu.VMEM((stack, total), BF16),
            pltpu.VMEM((held, total), BF16),
            pltpu.VMEM((total, held), BF16),
            pltpu.VMEM((held, LANES), F32),
            dma((3 + 2 * parts + 1,)),
            dma((tp - 1,)), dma((tp - 1,)),
            dma((n - 1,)), dma((n - 1,)),
            dma((n - 1,)), dma((n - 1,)),
            dma((n - 1,)), dma((n - 1,)),
            dma((tp - 1,)), dma((tp - 1,)),
        ],
        compiler_params=pltpu.CompilerParams(
            collective_id=0, has_side_effects=True, vmem_limit_bytes=60 * 1024 * 1024
        ),
        name="attention_step",
    )(
        frames,
        norm_gain.reshape(1, d_all),
        frame_session.reshape(1, sessions),
        owner_of.reshape(1, sessions),
        context_len.reshape(1, sessions),
        w_qkv,
        w_out,
        jnp.transpose(kv_cache, (0, 2, 1, 3)),
    )


def solution(mesh):
    in_specs = (
        P("sess", "tp"),
        P(),
        P(None, None, "tp"),
        P("tp", None),
        P(None, "sess", None, "tp"),
        P(),
        P(),
        P(),
    )
    out_specs = P("sess", "tp")
    return jax.shard_map(body, mesh=mesh, in_specs=in_specs, out_specs=out_specs, check_vma=False)
```

```python
import functools

import jax
import jax.numpy as jnp
from jax import lax
from jax.experimental import pallas as pl
from jax.experimental.pallas import tpu as pltpu
from jax.sharding import PartitionSpec as P

HD = 128
LANES = 128
MESH = pl.DeviceIdType.MESH
F32 = jnp.float32
BF16 = jnp.bfloat16


def quot(x, k):
    if k & (k - 1) == 0:
        return lax.shift_right_logical(x, jnp.full_like(x, k.bit_length() - 1))
    return lax.div(x, jnp.full_like(x, k))


def rest(x, k):
    return x - quot(x, k) * k


def iota(rows, cols, axis):
    return lax.broadcasted_iota(jnp.int32, (rows, cols), axis)


def one_hot(cond):
    return jnp.where(cond, 1.0, 0.0).astype(BF16)


def routing(me, n, heads, cap, msg, rows, slots, sessions, fs, owner, length):
    def pick(cond, values, axis):
        return jnp.sum(jnp.where(cond, values, 0.0), axis=axis, keepdims=True)

    i0, i1 = iota(sessions, sessions, 0), iota(sessions, sessions, 1)
    eye = i0 == i1

    def as_col(row):
        return pick(eye, row, 1)

    owner_c = as_col(owner)
    slot_c = pick((owner_c == owner) & (i1 < i0), 1.0, 1)
    match = i0 == fs
    row_owner = pick(match, owner_c, 0)
    row_slot = pick(match, slot_c, 0)
    row_len = pick(match, as_col(length), 0)
    row_owner_c, row_slot_c = as_col(row_owner), as_col(row_slot)
    block0, block1 = quot(i0, rows), quot(i1, rows)
    row_pair = pick((row_owner_c == row_owner) & (block0 == block1) & (i0 < i1), 1.0, 0)
    target = row_owner * cap + row_pair
    place = quot(iota(1, sessions, 1), rows).astype(F32) * cap + row_pair
    target_c, place_c = as_col(target), as_col(place)
    me_f = me.astype(F32)

    stack, total, held = heads * rows, n * msg, heads * slots

    def message_code(i):
        inner = rest(i, msg)
        return quot(inner, cap), (quot(i, msg) * cap + rest(inner, cap)).astype(F32)

    local = pick(
        iota(sessions, stack, 0) == me * rows + rest(iota(sessions, stack, 1), rows), target_c, 0
    )
    head_i, code = message_code(iota(total, stack, 0))
    send = one_hot((head_i == quot(iota(total, stack, 1), rows)) & (code == local))
    local_c = pick(
        iota(stack, sessions, 1) == me * rows + rest(iota(stack, sessions, 0), rows), target, 1
    )
    head_i, code = message_code(iota(stack, total, 1))
    unsend = one_hot((head_i == quot(iota(stack, total, 0), rows)) & (code == local_c))

    in_slot = (row_slot == rest(iota(held, sessions, 0), slots).astype(F32)) & (row_owner == me_f)
    _, code = message_code(iota(sessions, total, 1))
    spread = jnp.dot(one_hot(in_slot), one_hot(place_c == code), preferred_element_type=F32)
    head_i, _ = message_code(iota(held, total, 1))
    collect = jnp.where(head_i == quot(iota(held, total, 0), slots), spread, 0.0).astype(BF16)
    in_slot_t = (row_slot_c == rest(iota(sessions, held, 1), slots).astype(F32)) & (
        row_owner_c == me_f
    )
    _, code = message_code(iota(total, sessions, 0))
    spread = jnp.dot(one_hot(place == code), one_hot(in_slot_t), preferred_element_type=F32)
    head_i, _ = message_code(iota(total, held, 0))
    uncollect = jnp.where(head_i == quot(iota(total, held, 1), slots), spread, 0.0).astype(BF16)

    held_len = pick(in_slot, row_len, 1)
    lane = iota(held, LANES, 1)
    limit = jnp.where(
        rest(lane, slots) == rest(iota(held, LANES, 0), slots),
        held_len - quot(lane, slots).astype(F32),
        -1.0,
    )
    return send, unsend, collect, uncollect, limit


def kernel(
    dims,
    frames_hbm, gain_hbm, fs_hbm, owner_hbm, length_hbm, wqkv_hbm, wout_hbm, kv_hbm,
    out_ref,
    gain_v, fs_v, owner_v, length_v, w_v, wo_v, kv_v, fr_all, normed, q_send, q_recv, kv_send, kv_recv, r_send, r_recv,
    p_send, p_recv, scores, acc, send_m, unsend_m, collect_m, uncollect_m, limit_m,
    load_sem, ag_s, ag_r, q_s, q_r, kv_s, kv_r, r_s, r_r, p_s, p_r,
):
    n, tp, heads, cap, msg, rows, slots, ctx, tchunk, chunks, kc = dims
    dl = frames_hbm.shape[1]
    d_all = dl * tp
    me, mt = lax.axis_index("sess"), lax.axis_index("tp")
    sess_peer = [lax.rem(me + d, n) for d in range(n)]
    tp_peer = [lax.rem(mt + d, tp) for d in range(tp)]

    loads = []

    def load(src, dst):
        loads.append(pltpu.make_async_copy(src, dst, load_sem.at[len(loads)]))
        loads[-1].start()
        return loads[-1]

    barrier = pltpu.get_barrier_semaphore()
    for d in range(1, tp):
        pl.semaphore_signal(barrier, inc=1, device_id=(me, tp_peer[d]), device_id_type=MESH)
    for d in range(1, n):
        pl.semaphore_signal(barrier, inc=1, device_id=(sess_peer[d], mt), device_id_type=MESH)
    small = [
        load(fs_hbm, fs_v),
        load(owner_hbm, owner_v),
        load(length_hbm, length_v),
        load(gain_hbm, gain_v),
        load(frames_hbm, fr_all.at[mt]),
    ]
    w_load = [load(wqkv_hbm.at[c], w_v.at[c]) for c in range(3)]
    pl.semaphore_wait(barrier, n + tp - 2)

    def over_tp(src, dst, s, r, d):
        copy = pltpu.make_async_remote_copy(
            src_ref=src, dst_ref=dst, send_sem=s.at[d - 1], recv_sem=r.at[d - 1],
            device_id=(me, tp_peer[d]), device_id_type=MESH,
        )
        copy.start()
        return copy

    def over_sess(send, recv, s, r):
        copies = []
        for d in range(1, n):
            copy = pltpu.make_async_remote_copy(
                src_ref=send.at[sess_peer[d]], dst_ref=recv.at[me],
                send_sem=s.at[d - 1], recv_sem=r.at[d - 1],
                device_id=(sess_peer[d], mt), device_id_type=MESH,
            )
            copy.start()
            copies.append(copy)
        return copies

    ag = [over_tp(frames_hbm, fr_all.at[mt], ag_s, ag_r, d) for d in range(1, tp)]
    kv_load = []
    for c in range(2):
        parts = []
        for t0 in range(0, ctx, 4 * tchunk):
            size = min(4 * tchunk, ctx - t0)
            parts.append(
                load(kv_hbm.at[c, pl.ds(t0, size)], kv_v.at[c, pl.ds(t0, size)])
            )
        kv_load.append(parts)
    wo_load = load(wout_hbm, wo_v)

    pad = chunks * tchunk - ctx
    if pad:
        kv_v[:, ctx:] = jnp.zeros((2, pad) + kv_v.shape[2:], BF16)
    for copy in small:
        copy.wait()
    send_m[...], unsend_m[...], collect_m[...], uncollect_m[...], limit_m[...] = routing(
        me, n, heads, cap, msg, rows, slots, fs_v.shape[1],
        fs_v[...], owner_v[...].astype(F32), length_v[...].astype(F32),
    )

    for copy in ag:
        copy.wait()
    square = jnp.zeros((rows, 1), F32)
    for b in range(tp):
        wide = fr_all[b].astype(F32)
        square += jnp.sum(wide * wide, axis=1, keepdims=True)
    scale = lax.rsqrt(square * (1.0 / d_all) + 1e-05)
    gain = gain_v[...].astype(F32)
    for b in range(tp):
        for t in range(dl // LANES):
            col = b * dl + t * LANES
            part = fr_all[b, :, t * LANES : (t + 1) * LANES].astype(F32) * scale
            part = part * gain[col // LANES : col // LANES + 1]
            normed[col // kc, :, col % kc : col % kc + LANES] = part.astype(BF16)

    def project(c):
        w_load[c].wait()

        def step(k, total):
            block = w_v[c, pl.ds(pl.multiple_of(k * kc, kc), kc), :]
            return total + jnp.dot(normed[k], block, preferred_element_type=F32)

        out = lax.fori_loop(
            0, d_all // kc, step, jnp.zeros((rows, heads * HD), F32), unroll=4
        ).astype(BF16)
        stacked = jnp.concatenate([out[:, h * HD : (h + 1) * HD] for h in range(heads)], axis=0)
        placed = jnp.dot(send_m[...], stacked, preferred_element_type=F32)
        return placed.astype(BF16).reshape(n, msg, HD)

    q_send[...] = project(0)
    q_copies = over_sess(q_send, q_recv, q_s, q_r)
    q_recv[me] = q_send[me]
    kv_send[:, 0] = project(1)
    kv_send[:, 1] = project(2)
    kv_copies = over_sess(kv_send, kv_recv, kv_s, kv_r)
    kv_recv[me] = kv_send[me]

    def collected(block):
        return jnp.dot(
            collect_m[...], block.reshape(n * msg, HD), preferred_element_type=F32
        )

    factor = 1.0 / jnp.sqrt(jnp.float32(HD))
    held = heads * slots
    for copy in q_copies:
        copy.wait()
    query = collected(q_recv[...])
    head_row = quot(iota(held, HD, 0), slots)
    query_wide = jnp.concatenate(
        [jnp.where(head_row == h, query, 0.0) for h in range(heads)], axis=1
    ).astype(BF16)
    for copy in kv_load[0]:
        copy.wait()
    width = tchunk * slots
    tiles = width // LANES
    tile_t = LANES // slots
    limit = limit_m[...]

    def score_step(c, top):
        keys = kv_v[0, pl.ds(c * tchunk, tchunk)].reshape(width, heads * HD)
        s = lax.dot_general(
            query_wide, keys, (((1,), (1,)), ((), ())), preferred_element_type=F32
        )
        for k in range(tiles):
            edge = (c * tchunk + k * tile_t).astype(F32)
            tile = jnp.where(
                limit > edge, s[:, k * LANES : (k + 1) * LANES] * factor, -jnp.inf
            )
            scores[c, :, k * LANES : (k + 1) * LANES] = tile
            top = jnp.maximum(top, tile)
        return top

    top = lax.fori_loop(0, chunks, score_step, jnp.full((held, LANES), -jnp.inf, F32), unroll=2)

    for copy in kv_copies:
        copy.wait()
    new_key = collected(kv_recv[:, 0])
    new_value = collected(kv_recv[:, 1])
    own = jnp.sum(query * new_key, axis=1, keepdims=True) * factor
    top = jnp.maximum(jnp.max(top, axis=1, keepdims=True), own)
    top_wide = jnp.broadcast_to(top, (held, LANES))

    for copy in kv_load[1]:
        copy.wait()
    acc[...] = jnp.zeros_like(acc)

    def mix_step(c, total):
        weights = []
        for k in range(tiles):
            e = jnp.exp(scores[c, :, k * LANES : (k + 1) * LANES] - top_wide)
            total = total + e
            weights.append(e.astype(BF16))
        values = kv_v[1, pl.ds(c * tchunk, tchunk)].reshape(width, heads * HD)
        acc[...] += jnp.dot(
            jnp.concatenate(weights, axis=1), values, preferred_element_type=F32
        )
        return total

    total = lax.fori_loop(0, chunks, mix_step, jnp.zeros((held, LANES), F32), unroll=2)
    own_exp = jnp.exp(own - top)
    inverse = 1.0 / (jnp.sum(total, axis=1, keepdims=True) + own_exp)
    own_weight = own_exp.astype(BF16).astype(F32)
    mixed = jnp.concatenate(
        [acc[h * slots : (h + 1) * slots, h * HD : (h + 1) * HD] for h in range(heads)], axis=0
    )
    attended = ((mixed + own_weight * new_value) * inverse).astype(BF16)
    r_send[...] = (
        jnp.dot(uncollect_m[...], attended, preferred_element_type=F32)
        .astype(BF16)
        .reshape(n, msg, HD)
    )
    r_copies = over_sess(r_send, r_recv, r_s, r_r)
    r_recv[me] = r_send[me]
    wo_load.wait()
    for copy in r_copies:
        copy.wait()
    back = jnp.dot(
        unsend_m[...], r_recv[...].reshape(n * msg, HD), preferred_element_type=F32
    ).astype(BF16)
    mine = jnp.concatenate([back[h * rows : (h + 1) * rows] for h in range(heads)], axis=1)

    def branch(dest):
        block = wo_v[:, pl.ds(pl.multiple_of(dest * dl, dl), dl)]
        return jnp.dot(mine, block, preferred_element_type=F32)

    p_copies = []
    for d in range(1, tp):
        p_send[d - 1] = branch(tp_peer[d]).astype(BF16)
        p_copies.append(over_tp(p_send.at[d - 1], p_recv.at[d - 1], p_s, p_r, d))
    result = branch(mt)
    for d in range(1, tp):
        p_copies[d - 1].wait()
        result = result + p_recv[d - 1].astype(F32)
    out_ref[...] = (fr_all[mt].astype(F32) + result).astype(BF16)


def body(frames, norm_gain, w_qkv, w_out, kv_cache, frame_session, owner_of, context_len):
    n, tp = lax.axis_size("sess"), lax.axis_size("tp")
    rows, dl = frames.shape
    d_all, head_cols = w_qkv.shape[1:]
    slots, ctx = kv_cache.shape[1:3]
    sessions = frame_session.shape[0]
    heads = head_cols // HD
    cap = (slots + n - 1) // n
    msg = (heads * cap + 15) // 16 * 16
    tchunk = 1024 // slots
    chunks = (ctx + tchunk - 1) // tchunk
    kc = min(512, dl)
    held, total, stack = heads * slots, n * msg, heads * rows
    parts = (ctx + 4 * tchunk - 1) // (4 * tchunk)
    dims = (n, tp, heads, cap, msg, rows, slots, ctx, tchunk, chunks, kc)
    vmem = pl.BlockSpec(memory_space=pltpu.VMEM)
    hbm = pl.BlockSpec(memory_space=pl.ANY)
    dma = pltpu.SemaphoreType.DMA
    return pl.pallas_call(
        functools.partial(kernel, dims),
        out_shape=pltpu.VMEM((rows, dl), BF16),
        in_specs=[hbm] * 8,
        out_specs=vmem,
        scratch_shapes=[
            pltpu.VMEM((d_all // LANES, LANES), BF16),
            pltpu.VMEM((1, sessions), jnp.int32),
            pltpu.VMEM((1, sessions), jnp.int32),
            pltpu.VMEM((1, sessions), jnp.int32),
            pltpu.VMEM((3, d_all, head_cols), BF16),
            pltpu.VMEM((head_cols, d_all), BF16),
            pltpu.VMEM((2, chunks * tchunk, slots, head_cols), BF16),
            pltpu.VMEM((tp, rows, dl), BF16),
            pltpu.VMEM((d_all // kc, rows, kc), BF16),
            pltpu.VMEM((n, msg, HD), BF16),
            pltpu.VMEM((n, msg, HD), BF16),
            pltpu.VMEM((n, 2, msg, HD), BF16),
            pltpu.VMEM((n, 2, msg, HD), BF16),
            pltpu.VMEM((n, msg, HD), BF16),
            pltpu.VMEM((n, msg, HD), BF16),
            pltpu.VMEM((tp - 1, rows, dl), BF16),
            pltpu.VMEM((tp - 1, rows, dl), BF16),
            pltpu.VMEM((chunks, held, tchunk * slots), F32),
            pltpu.VMEM((held, head_cols), F32),
            pltpu.VMEM((total, stack), BF16),
            pltpu.VMEM((stack, total), BF16),
            pltpu.VMEM((held, total), BF16),
            pltpu.VMEM((total, held), BF16),
            pltpu.VMEM((held, LANES), F32),
            dma((5 + 3 + 2 * parts + 1,)),
            dma((tp - 1,)), dma((tp - 1,)),
            dma((n - 1,)), dma((n - 1,)),
            dma((n - 1,)), dma((n - 1,)),
            dma((n - 1,)), dma((n - 1,)),
            dma((tp - 1,)), dma((tp - 1,)),
        ],
        compiler_params=pltpu.CompilerParams(
            collective_id=0, has_side_effects=True, vmem_limit_bytes=60 * 1024 * 1024
        ),
        name="attention_step",
    )(
        frames,
        norm_gain.reshape(d_all // LANES, LANES),
        frame_session.reshape(1, sessions),
        owner_of.reshape(1, sessions),
        context_len.reshape(1, sessions),
        w_qkv,
        w_out,
        jnp.transpose(kv_cache, (0, 2, 1, 3)),
    )


def solution(mesh):
    in_specs = (
        P("sess", "tp"),
        P(),
        P(None, None, "tp"),
        P("tp", None),
        P(None, "sess", None, "tp"),
        P(),
        P(),
        P(),
    )
    out_specs = P("sess", "tp")
    return jax.shard_map(body, mesh=mesh, in_specs=in_specs, out_specs=out_specs, check_vma=False)
```

```python
import functools

import jax
import jax.numpy as jnp
from jax import lax
from jax.experimental import pallas as pl
from jax.experimental.pallas import tpu as pltpu
from jax.sharding import PartitionSpec as P

HD = 128
LANES = 128
MESH = pl.DeviceIdType.MESH
F32 = jnp.float32
BF16 = jnp.bfloat16


def quot(x, k):
    if k & (k - 1) == 0:
        return lax.shift_right_logical(x, jnp.full_like(x, k.bit_length() - 1))
    return lax.div(x, jnp.full_like(x, k))


def rest(x, k):
    return x - quot(x, k) * k


def iota(rows, cols, axis):
    return lax.broadcasted_iota(jnp.int32, (rows, cols), axis)


def one_hot(cond):
    return jnp.where(cond, 1.0, 0.0).astype(BF16)


def routing(me, n, heads, cap, msg, rows, slots, sessions, fs, owner, length):
    def pick(cond, values, axis):
        return jnp.sum(jnp.where(cond, values, 0.0), axis=axis, keepdims=True)

    i0, i1 = iota(sessions, sessions, 0), iota(sessions, sessions, 1)
    eye = i0 == i1

    def as_col(row):
        return pick(eye, row, 1)

    owner_c = as_col(owner)
    slot_c = pick((owner_c == owner) & (i1 < i0), 1.0, 1)
    match = i0 == fs
    row_owner = pick(match, owner_c, 0)
    row_slot = pick(match, slot_c, 0)
    row_len = pick(match, as_col(length), 0)
    row_owner_c, row_slot_c = as_col(row_owner), as_col(row_slot)
    block0, block1 = quot(i0, rows), quot(i1, rows)
    row_pair = pick((row_owner_c == row_owner) & (block0 == block1) & (i0 < i1), 1.0, 0)
    target = row_owner * cap + row_pair
    place = quot(iota(1, sessions, 1), rows).astype(F32) * cap + row_pair
    target_c, place_c = as_col(target), as_col(place)
    me_f = me.astype(F32)

    stack, total, held = heads * rows, n * msg, heads * slots

    def message_code(i):
        inner = rest(i, msg)
        return quot(inner, cap), (quot(i, msg) * cap + rest(inner, cap)).astype(F32)

    local = pick(
        iota(sessions, stack, 0) == me * rows + rest(iota(sessions, stack, 1), rows), target_c, 0
    )
    head_i, code = message_code(iota(total, stack, 0))
    send = one_hot((head_i == quot(iota(total, stack, 1), rows)) & (code == local))
    local_c = pick(
        iota(stack, sessions, 1) == me * rows + rest(iota(stack, sessions, 0), rows), target, 1
    )
    head_i, code = message_code(iota(stack, total, 1))
    unsend = one_hot((head_i == quot(iota(stack, total, 0), rows)) & (code == local_c))

    in_slot = (row_slot == rest(iota(held, sessions, 0), slots).astype(F32)) & (row_owner == me_f)
    _, code = message_code(iota(sessions, total, 1))
    spread = jnp.dot(one_hot(in_slot), one_hot(place_c == code), preferred_element_type=F32)
    head_i, _ = message_code(iota(held, total, 1))
    collect = jnp.where(head_i == quot(iota(held, total, 0), slots), spread, 0.0).astype(BF16)
    in_slot_t = (row_slot_c == rest(iota(sessions, held, 1), slots).astype(F32)) & (
        row_owner_c == me_f
    )
    _, code = message_code(iota(total, sessions, 0))
    spread = jnp.dot(one_hot(place == code), one_hot(in_slot_t), preferred_element_type=F32)
    head_i, _ = message_code(iota(total, held, 0))
    uncollect = jnp.where(head_i == quot(iota(total, held, 1), slots), spread, 0.0).astype(BF16)

    held_len = pick(in_slot, row_len, 1)
    lane = iota(held, LANES, 1)
    limit = jnp.where(
        rest(lane, slots) == rest(iota(held, LANES, 0), slots),
        held_len - quot(lane, slots).astype(F32),
        -1.0,
    )
    return send, unsend, collect, uncollect, limit


def kernel(
    dims,
    frames_hbm, gain_hbm, fs_hbm, owner_hbm, length_hbm, wqkv_hbm, wout_hbm, kv_hbm,
    out_ref,
    gain_v, fs_v, owner_v, length_v, w_v, wo_v, kv_v, fr_all, normed, q_send, q_recv, kv_send, kv_recv, r_send, r_recv,
    p_send, p_recv, scores, acc, send_m, unsend_m, collect_m, uncollect_m, limit_m,
    load_sem, ag_s, ag_r, q_s, q_r, kv_s, kv_r, r_s, r_r, p_s, p_r,
):
    n, tp, heads, cap, msg, rows, slots, ctx, tchunk, chunks, kc = dims
    dl = frames_hbm.shape[1]
    d_all = dl * tp
    me, mt = lax.axis_index("sess"), lax.axis_index("tp")
    sess_peer = [lax.rem(me + d, n) for d in range(n)]
    tp_peer = [lax.rem(mt + d, tp) for d in range(tp)]

    loads = []

    def load(src, dst):
        loads.append(pltpu.make_async_copy(src, dst, load_sem.at[len(loads)]))
        loads[-1].start()
        return loads[-1]

    barrier = pltpu.get_barrier_semaphore()
    for d in range(1, tp):
        pl.semaphore_signal(barrier, inc=1, device_id=(me, tp_peer[d]), device_id_type=MESH)
    for d in range(1, n):
        pl.semaphore_signal(barrier, inc=1, device_id=(sess_peer[d], mt), device_id_type=MESH)
    small = [
        load(fs_hbm, fs_v),
        load(owner_hbm, owner_v),
        load(length_hbm, length_v),
        load(gain_hbm, gain_v),
        load(frames_hbm, fr_all.at[mt]),
    ]
    w_load = [load(wqkv_hbm.at[0], w_v.at[0])]
    pl.semaphore_wait(barrier, n + tp - 2)

    def over_tp(src, dst, s, r, d):
        copy = pltpu.make_async_remote_copy(
            src_ref=src, dst_ref=dst, send_sem=s.at[d - 1], recv_sem=r.at[d - 1],
            device_id=(me, tp_peer[d]), device_id_type=MESH,
        )
        copy.start()
        return copy

    def over_sess(send, recv, s, r):
        copies = []
        for d in range(1, n):
            copy = pltpu.make_async_remote_copy(
                src_ref=send.at[sess_peer[d]], dst_ref=recv.at[me],
                send_sem=s.at[d - 1], recv_sem=r.at[d - 1],
                device_id=(sess_peer[d], mt), device_id_type=MESH,
            )
            copy.start()
            copies.append(copy)
        return copies

    ag = [over_tp(frames_hbm, fr_all.at[mt], ag_s, ag_r, d) for d in range(1, tp)]
    w_load += [load(wqkv_hbm.at[c], w_v.at[c]) for c in (1, 2)]

    def load_cache(c):
        parts = []
        for t0 in range(0, ctx, 4 * tchunk):
            span = pl.ds(t0, min(4 * tchunk, ctx - t0))
            parts.append(load(kv_hbm.at[c, span], kv_v.at[c, span]))
        return parts

    def over_cache(parts, step, carry):
        for i, copy in enumerate(parts):
            copy.wait()
            carry = lax.fori_loop(4 * i, min(4 * i + 4, chunks), step, carry, unroll=2)
        return carry

    key_load = load_cache(0)
    pad = chunks * tchunk - ctx
    if pad:
        kv_v[:, ctx:] = jnp.zeros((2, pad) + kv_v.shape[2:], BF16)
    for copy in small:
        copy.wait()
    send_m[...], unsend_m[...], collect_m[...], uncollect_m[...], limit_m[...] = routing(
        me, n, heads, cap, msg, rows, slots, fs_v.shape[1],
        fs_v[...], owner_v[...].astype(F32), length_v[...].astype(F32),
    )

    for copy in ag:
        copy.wait()
    square = jnp.zeros((rows, 1), F32)
    for b in range(tp):
        wide = fr_all[b].astype(F32)
        square += jnp.sum(wide * wide, axis=1, keepdims=True)
    scale = lax.rsqrt(square * (1.0 / d_all) + 1e-05)
    gain = gain_v[...].astype(F32)
    for b in range(tp):
        for t in range(dl // LANES):
            col = b * dl + t * LANES
            part = fr_all[b, :, t * LANES : (t + 1) * LANES].astype(F32) * scale
            part = part * gain[col // LANES : col // LANES + 1]
            normed[col // kc, :, col % kc : col % kc + LANES] = part.astype(BF16)

    def project(c):
        w_load[c].wait()

        def step(k, total):
            block = w_v[c, pl.ds(pl.multiple_of(k * kc, kc), kc), :]
            return total + jnp.dot(normed[k], block, preferred_element_type=F32)

        out = lax.fori_loop(
            0, d_all // kc, step, jnp.zeros((rows, heads * HD), F32), unroll=4
        ).astype(BF16)
        stacked = jnp.concatenate([out[:, h * HD : (h + 1) * HD] for h in range(heads)], axis=0)
        placed = jnp.dot(send_m[...], stacked, preferred_element_type=F32)
        return placed.astype(BF16).reshape(n, msg, HD)

    q_send[...] = project(0)
    q_copies = over_sess(q_send, q_recv, q_s, q_r)
    value_load = load_cache(1)
    q_recv[me] = q_send[me]
    kv_send[:, 0] = project(1)
    kv_send[:, 1] = project(2)
    kv_copies = over_sess(kv_send, kv_recv, kv_s, kv_r)
    wo_load = load(wout_hbm, wo_v)
    kv_recv[me] = kv_send[me]

    def collected(block):
        return jnp.dot(
            collect_m[...], block.reshape(n * msg, HD), preferred_element_type=F32
        )

    factor = 1.0 / jnp.sqrt(jnp.float32(HD))
    held = heads * slots
    for copy in q_copies:
        copy.wait()
    query = collected(q_recv[...])
    head_row = quot(iota(held, HD, 0), slots)
    query_wide = jnp.concatenate(
        [jnp.where(head_row == h, query, 0.0) for h in range(heads)], axis=1
    ).astype(BF16)
    width = tchunk * slots
    tiles = width // LANES
    tile_t = LANES // slots
    limit = limit_m[...]

    def score_step(c, top):
        keys = kv_v[0, pl.ds(c * tchunk, tchunk)].reshape(width, heads * HD)
        s = lax.dot_general(
            query_wide, keys, (((1,), (1,)), ((), ())), preferred_element_type=F32
        )
        for k in range(tiles):
            edge = (c * tchunk + k * tile_t).astype(F32)
            tile = jnp.where(
                limit > edge, s[:, k * LANES : (k + 1) * LANES] * factor, -jnp.inf
            )
            scores[c, :, k * LANES : (k + 1) * LANES] = tile
            top = jnp.maximum(top, tile)
        return top

    top = over_cache(key_load, score_step, jnp.full((held, LANES), -jnp.inf, F32))

    for copy in kv_copies:
        copy.wait()
    new_key = collected(kv_recv[:, 0])
    new_value = collected(kv_recv[:, 1])
    own = jnp.sum(query * new_key, axis=1, keepdims=True) * factor
    top = jnp.maximum(jnp.max(top, axis=1, keepdims=True), own)
    top_wide = jnp.broadcast_to(top, (held, LANES))

    acc[...] = jnp.zeros_like(acc)

    def mix_step(c, total):
        weights = []
        for k in range(tiles):
            e = jnp.exp(scores[c, :, k * LANES : (k + 1) * LANES] - top_wide)
            total = total + e
            weights.append(e.astype(BF16))
        values = kv_v[1, pl.ds(c * tchunk, tchunk)].reshape(width, heads * HD)
        acc[...] += jnp.dot(
            jnp.concatenate(weights, axis=1), values, preferred_element_type=F32
        )
        return total

    total = over_cache(value_load, mix_step, jnp.zeros((held, LANES), F32))
    own_exp = jnp.exp(own - top)
    inverse = 1.0 / (jnp.sum(total, axis=1, keepdims=True) + own_exp)
    own_weight = own_exp.astype(BF16).astype(F32)
    mixed = jnp.concatenate(
        [acc[h * slots : (h + 1) * slots, h * HD : (h + 1) * HD] for h in range(heads)], axis=0
    )
    attended = ((mixed + own_weight * new_value) * inverse).astype(BF16)
    r_send[...] = (
        jnp.dot(uncollect_m[...], attended, preferred_element_type=F32)
        .astype(BF16)
        .reshape(n, msg, HD)
    )
    r_copies = over_sess(r_send, r_recv, r_s, r_r)
    r_recv[me] = r_send[me]
    wo_load.wait()
    for copy in r_copies:
        copy.wait()
    back = jnp.dot(
        unsend_m[...], r_recv[...].reshape(n * msg, HD), preferred_element_type=F32
    ).astype(BF16)
    mine = jnp.concatenate([back[h * rows : (h + 1) * rows] for h in range(heads)], axis=1)

    def branch(dest):
        block = wo_v[:, pl.ds(pl.multiple_of(dest * dl, dl), dl)]
        return jnp.dot(mine, block, preferred_element_type=F32)

    p_copies = []
    for d in range(1, tp):
        p_send[d - 1] = branch(tp_peer[d]).astype(BF16)
        p_copies.append(over_tp(p_send.at[d - 1], p_recv.at[d - 1], p_s, p_r, d))
    result = branch(mt)
    for d in range(1, tp):
        p_copies[d - 1].wait()
        result = result + p_recv[d - 1].astype(F32)
    out_ref[...] = (fr_all[mt].astype(F32) + result).astype(BF16)


def body(frames, norm_gain, w_qkv, w_out, kv_cache, frame_session, owner_of, context_len):
    n, tp = lax.axis_size("sess"), lax.axis_size("tp")
    rows, dl = frames.shape
    d_all, head_cols = w_qkv.shape[1:]
    slots, ctx = kv_cache.shape[1:3]
    sessions = frame_session.shape[0]
    heads = head_cols // HD
    cap = (slots + n - 1) // n
    msg = (heads * cap + 15) // 16 * 16
    tchunk = 1024 // slots
    chunks = (ctx + tchunk - 1) // tchunk
    kc = min(512, dl)
    held, total, stack = heads * slots, n * msg, heads * rows
    parts = (ctx + 4 * tchunk - 1) // (4 * tchunk)
    dims = (n, tp, heads, cap, msg, rows, slots, ctx, tchunk, chunks, kc)
    vmem = pl.BlockSpec(memory_space=pltpu.VMEM)
    hbm = pl.BlockSpec(memory_space=pl.ANY)
    dma = pltpu.SemaphoreType.DMA
    return pl.pallas_call(
        functools.partial(kernel, dims),
        out_shape=pltpu.VMEM((rows, dl), BF16),
        in_specs=[hbm] * 8,
        out_specs=vmem,
        scratch_shapes=[
            pltpu.VMEM((d_all // LANES, LANES), BF16),
            pltpu.VMEM((1, sessions), jnp.int32),
            pltpu.VMEM((1, sessions), jnp.int32),
            pltpu.VMEM((1, sessions), jnp.int32),
            pltpu.VMEM((3, d_all, head_cols), BF16),
            pltpu.VMEM((head_cols, d_all), BF16),
            pltpu.VMEM((2, chunks * tchunk, slots, head_cols), BF16),
            pltpu.VMEM((tp, rows, dl), BF16),
            pltpu.VMEM((d_all // kc, rows, kc), BF16),
            pltpu.VMEM((n, msg, HD), BF16),
            pltpu.VMEM((n, msg, HD), BF16),
            pltpu.VMEM((n, 2, msg, HD), BF16),
            pltpu.VMEM((n, 2, msg, HD), BF16),
            pltpu.VMEM((n, msg, HD), BF16),
            pltpu.VMEM((n, msg, HD), BF16),
            pltpu.VMEM((tp - 1, rows, dl), BF16),
            pltpu.VMEM((tp - 1, rows, dl), BF16),
            pltpu.VMEM((chunks, held, tchunk * slots), F32),
            pltpu.VMEM((held, head_cols), F32),
            pltpu.VMEM((total, stack), BF16),
            pltpu.VMEM((stack, total), BF16),
            pltpu.VMEM((held, total), BF16),
            pltpu.VMEM((total, held), BF16),
            pltpu.VMEM((held, LANES), F32),
            dma((5 + 3 + 2 * parts + 1,)),
            dma((tp - 1,)), dma((tp - 1,)),
            dma((n - 1,)), dma((n - 1,)),
            dma((n - 1,)), dma((n - 1,)),
            dma((n - 1,)), dma((n - 1,)),
            dma((tp - 1,)), dma((tp - 1,)),
        ],
        compiler_params=pltpu.CompilerParams(
            collective_id=0, has_side_effects=True, vmem_limit_bytes=60 * 1024 * 1024
        ),
        name="attention_step",
    )(
        frames,
        norm_gain.reshape(d_all // LANES, LANES),
        frame_session.reshape(1, sessions),
        owner_of.reshape(1, sessions),
        context_len.reshape(1, sessions),
        w_qkv,
        w_out,
        jnp.transpose(kv_cache, (0, 2, 1, 3)),
    )


def solution(mesh):
    in_specs = (
        P("sess", "tp"),
        P(),
        P(None, None, "tp"),
        P("tp", None),
        P(None, "sess", None, "tp"),
        P(),
        P(),
        P(),
    )
    out_specs = P("sess", "tp")
    return jax.shard_map(body, mesh=mesh, in_specs=in_specs, out_specs=out_specs, check_vma=False)
```

```python
import functools

import jax
import jax.numpy as jnp
from jax import lax
from jax.experimental import pallas as pl
from jax.experimental.pallas import tpu as pltpu
from jax.sharding import PartitionSpec as P

HD = 128
LANES = 128
MESH = pl.DeviceIdType.MESH
F32 = jnp.float32
BF16 = jnp.bfloat16


def quot(x, k):
    if k & (k - 1) == 0:
        return lax.shift_right_logical(x, jnp.full_like(x, k.bit_length() - 1))
    return lax.div(x, jnp.full_like(x, k))


def rest(x, k):
    return x - quot(x, k) * k


def iota(rows, cols, axis):
    return lax.broadcasted_iota(jnp.int32, (rows, cols), axis)


def one_hot(cond):
    return jnp.where(cond, 1.0, 0.0).astype(BF16)


def routing(me, n, heads, cap, msg, rows, slots, sessions, fs, owner, length):
    def pick(cond, values, axis):
        return jnp.sum(jnp.where(cond, values, 0.0), axis=axis, keepdims=True)

    i0, i1 = iota(sessions, sessions, 0), iota(sessions, sessions, 1)
    eye = i0 == i1

    def as_col(row):
        return pick(eye, row, 1)

    owner_c = as_col(owner)
    slot_c = pick((owner_c == owner) & (i1 < i0), 1.0, 1)
    match = i0 == fs
    row_owner = pick(match, owner_c, 0)
    row_slot = pick(match, slot_c, 0)
    row_len = pick(match, as_col(length), 0)
    row_owner_c, row_slot_c = as_col(row_owner), as_col(row_slot)
    block0, block1 = quot(i0, rows), quot(i1, rows)
    row_pair = pick((row_owner_c == row_owner) & (block0 == block1) & (i0 < i1), 1.0, 0)
    target = row_owner * cap + row_pair
    place = quot(iota(1, sessions, 1), rows).astype(F32) * cap + row_pair
    target_c, place_c = as_col(target), as_col(place)
    me_f = me.astype(F32)

    stack, total, held = heads * rows, n * msg, heads * slots

    def message_code(i):
        inner = rest(i, msg)
        return quot(inner, cap), (quot(i, msg) * cap + rest(inner, cap)).astype(F32)

    local = pick(
        iota(sessions, stack, 0) == me * rows + rest(iota(sessions, stack, 1), rows), target_c, 0
    )
    head_i, code = message_code(iota(total, stack, 0))
    send = one_hot((head_i == quot(iota(total, stack, 1), rows)) & (code == local))
    local_c = pick(
        iota(stack, sessions, 1) == me * rows + rest(iota(stack, sessions, 0), rows), target, 1
    )
    head_i, code = message_code(iota(stack, total, 1))
    unsend = one_hot((head_i == quot(iota(stack, total, 0), rows)) & (code == local_c))

    in_slot = (row_slot == rest(iota(held, sessions, 0), slots).astype(F32)) & (row_owner == me_f)
    _, code = message_code(iota(sessions, total, 1))
    spread = jnp.dot(one_hot(in_slot), one_hot(place_c == code), preferred_element_type=F32)
    head_i, _ = message_code(iota(held, total, 1))
    collect = jnp.where(head_i == quot(iota(held, total, 0), slots), spread, 0.0).astype(BF16)
    in_slot_t = (row_slot_c == rest(iota(sessions, held, 1), slots).astype(F32)) & (
        row_owner_c == me_f
    )
    _, code = message_code(iota(total, sessions, 0))
    spread = jnp.dot(one_hot(place == code), one_hot(in_slot_t), preferred_element_type=F32)
    head_i, _ = message_code(iota(total, held, 0))
    uncollect = jnp.where(head_i == quot(iota(total, held, 1), slots), spread, 0.0).astype(BF16)

    held_len = pick(in_slot, row_len, 1)
    lane = iota(held, LANES, 1)
    limit = jnp.where(
        rest(lane, slots) == rest(iota(held, LANES, 0), slots),
        held_len - quot(lane, slots).astype(F32),
        -1.0,
    )
    return send, unsend, collect, uncollect, limit


def kernel(
    dims,
    frames_hbm, gain_hbm, fs_hbm, owner_hbm, length_hbm, wqkv_hbm, wout_hbm, kv_hbm,
    out_ref,
    gain_v, fs_v, owner_v, length_v, w_v, wo_v, kv_v, fr_all, normed, q_send, q_recv, kv_send, kv_recv, r_send, r_recv,
    p_send, p_recv, scores, acc, send_m, unsend_m, collect_m, uncollect_m, limit_m,
    load_sem, ag_s, ag_r, q_s, q_r, kv_s, kv_r, r_s, r_r, p_s, p_r,
):
    n, tp, heads, cap, msg, rows, slots, ctx, tchunk, chunks = dims
    dl = frames_hbm.shape[1]
    d_all = dl * tp
    me, mt = lax.axis_index("sess"), lax.axis_index("tp")
    sess_peer = [lax.rem(me + d, n) for d in range(n)]
    tp_peer = [lax.rem(mt + d, tp) for d in range(tp)]

    loads = []

    def load(src, dst):
        loads.append(pltpu.make_async_copy(src, dst, load_sem.at[len(loads)]))
        loads[-1].start()
        return loads[-1]

    barrier = pltpu.get_barrier_semaphore()
    for d in range(1, tp):
        pl.semaphore_signal(barrier, inc=1, device_id=(me, tp_peer[d]), device_id_type=MESH)
    for d in range(1, n):
        pl.semaphore_signal(barrier, inc=1, device_id=(sess_peer[d], mt), device_id_type=MESH)
    small = [
        load(fs_hbm, fs_v),
        load(owner_hbm, owner_v),
        load(length_hbm, length_v),
        load(gain_hbm, gain_v),
        load(frames_hbm, fr_all.at[mt]),
    ]
    w_load = [load(wqkv_hbm.at[0], w_v.at[0])]
    pl.semaphore_wait(barrier, n + tp - 2)

    def over_tp(src, dst, s, r, d):
        copy = pltpu.make_async_remote_copy(
            src_ref=src, dst_ref=dst, send_sem=s.at[d - 1], recv_sem=r.at[d - 1],
            device_id=(me, tp_peer[d]), device_id_type=MESH,
        )
        copy.start()
        return copy

    def over_sess(send, recv, s, r):
        copies = []
        for d in range(1, n):
            copy = pltpu.make_async_remote_copy(
                src_ref=send.at[sess_peer[d]], dst_ref=recv.at[me],
                send_sem=s.at[d - 1], recv_sem=r.at[d - 1],
                device_id=(sess_peer[d], mt), device_id_type=MESH,
            )
            copy.start()
            copies.append(copy)
        return copies

    ag = [over_tp(frames_hbm, fr_all.at[mt], ag_s, ag_r, d) for d in range(1, tp)]
    w_load += [load(wqkv_hbm.at[c], w_v.at[c]) for c in (1, 2)]

    def load_cache(c):
        parts = []
        for t0 in range(0, ctx, 4 * tchunk):
            span = pl.ds(t0, min(4 * tchunk, ctx - t0))
            parts.append(load(kv_hbm.at[c, span], kv_v.at[c, span]))
        return parts

    key_load = load_cache(0)
    pad = chunks * tchunk - ctx
    if pad:
        kv_v[:, ctx:] = jnp.zeros((2, pad) + kv_v.shape[2:], BF16)
    for copy in small:
        copy.wait()
    send_m[...], unsend_m[...], collect_m[...], uncollect_m[...], limit_m[...] = routing(
        me, n, heads, cap, msg, rows, slots, fs_v.shape[1],
        fs_v[...], owner_v[...].astype(F32), length_v[...].astype(F32),
    )

    for copy in ag:
        copy.wait()
    square = jnp.zeros((rows, 1), F32)
    for b in range(tp):
        wide = fr_all[b].astype(F32)
        square += jnp.sum(wide * wide, axis=1, keepdims=True)
    scale = lax.rsqrt(square * (1.0 / d_all) + 1e-05)
    gain = gain_v[...].astype(F32)
    for b in range(tp):
        for t in range(dl // LANES):
            col = b * dl + t * LANES
            part = fr_all[b, :, t * LANES : (t + 1) * LANES].astype(F32) * scale
            part = part * gain[col // LANES : col // LANES + 1]
            normed[:, col : col + LANES] = part.astype(BF16)

    def project(c):
        w_load[c].wait()

        out = jnp.dot(normed[...], w_v[c], preferred_element_type=F32).astype(BF16)
        stacked = jnp.concatenate([out[:, h * HD : (h + 1) * HD] for h in range(heads)], axis=0)
        placed = jnp.dot(send_m[...], stacked, preferred_element_type=F32)
        return placed.astype(BF16).reshape(n, msg, HD)

    q_send[...] = project(0)
    q_copies = over_sess(q_send, q_recv, q_s, q_r)
    value_load = load_cache(1)
    q_recv[me] = q_send[me]
    kv_send[:, 0] = project(1)
    kv_send[:, 1] = project(2)
    kv_copies = over_sess(kv_send, kv_recv, kv_s, kv_r)
    wo_load = load(wout_hbm, wo_v)
    kv_recv[me] = kv_send[me]

    def collected(block):
        return jnp.dot(
            collect_m[...], block.reshape(n * msg, HD), preferred_element_type=F32
        )

    factor = 1.0 / jnp.sqrt(jnp.float32(HD))
    held = heads * slots
    for copy in q_copies:
        copy.wait()
    query = collected(q_recv[...])
    head_row = quot(iota(held, HD, 0), slots)
    query_wide = jnp.concatenate(
        [jnp.where(head_row == h, query, 0.0) for h in range(heads)], axis=1
    ).astype(BF16)
    width = tchunk * slots
    tiles = width // LANES
    tile_t = LANES // slots
    limit = limit_m[...]

    def score_step(c, top):
        keys = kv_v[0, pl.ds(c * tchunk, tchunk)].reshape(width, heads * HD)
        s = lax.dot_general(
            query_wide, keys, (((1,), (1,)), ((), ())), preferred_element_type=F32
        )
        for k in range(tiles):
            edge = float(c * tchunk + k * tile_t)
            tile = jnp.where(
                limit > edge, s[:, k * LANES : (k + 1) * LANES] * factor, -jnp.inf
            )
            scores[c, :, k * LANES : (k + 1) * LANES] = tile
            top = jnp.maximum(top, tile)
        return top

    top = jnp.full((held, LANES), -jnp.inf, F32)
    for i, copy in enumerate(key_load):
        copy.wait()
        for c in range(4 * i, min(4 * i + 4, chunks)):
            top = score_step(c, top)

    for copy in kv_copies:
        copy.wait()
    new_key = collected(kv_recv[:, 0])
    new_value = collected(kv_recv[:, 1])
    own = jnp.sum(query * new_key, axis=1, keepdims=True) * factor
    top = jnp.maximum(jnp.max(top, axis=1, keepdims=True), own)
    top_wide = jnp.broadcast_to(top, (held, LANES))

    total = jnp.zeros((held, LANES), F32)
    for i, copy in enumerate(value_load):
        weights = []
        for c in range(4 * i, min(4 * i + 4, chunks)):
            for k in range(tiles):
                e = jnp.exp(scores[c, :, k * LANES : (k + 1) * LANES] - top_wide)
                total = total + e
                weights.append(e.astype(BF16))
        copy.wait()
        span = len(weights) * LANES
        values = kv_v[1, pl.ds(4 * i * tchunk, span // slots)].reshape(span, heads * HD)
        part = jnp.dot(jnp.concatenate(weights, axis=1), values, preferred_element_type=F32)
        acc[...] = part if i == 0 else acc[...] + part
    own_exp = jnp.exp(own - top)
    inverse = 1.0 / (jnp.sum(total, axis=1, keepdims=True) + own_exp)
    own_weight = own_exp.astype(BF16).astype(F32)
    mixed = jnp.concatenate(
        [acc[h * slots : (h + 1) * slots, h * HD : (h + 1) * HD] for h in range(heads)], axis=0
    )
    attended = ((mixed + own_weight * new_value) * inverse).astype(BF16)
    r_send[...] = (
        jnp.dot(uncollect_m[...], attended, preferred_element_type=F32)
        .astype(BF16)
        .reshape(n, msg, HD)
    )
    r_copies = over_sess(r_send, r_recv, r_s, r_r)
    r_recv[me] = r_send[me]
    wo_load.wait()
    for copy in r_copies:
        copy.wait()
    back = jnp.dot(
        unsend_m[...], r_recv[...].reshape(n * msg, HD), preferred_element_type=F32
    ).astype(BF16)
    mine = jnp.concatenate([back[h * rows : (h + 1) * rows] for h in range(heads)], axis=1)

    def branch(dest):
        block = wo_v[:, pl.ds(pl.multiple_of(dest * dl, dl), dl)]
        return jnp.dot(mine, block, preferred_element_type=F32)

    p_copies = []
    for d in range(1, tp):
        p_send[d - 1] = branch(tp_peer[d]).astype(BF16)
        p_copies.append(over_tp(p_send.at[d - 1], p_recv.at[d - 1], p_s, p_r, d))
    result = branch(mt)
    for d in range(1, tp):
        p_copies[d - 1].wait()
        result = result + p_recv[d - 1].astype(F32)
    out_ref[...] = (fr_all[mt].astype(F32) + result).astype(BF16)


def body(frames, norm_gain, w_qkv, w_out, kv_cache, frame_session, owner_of, context_len):
    n, tp = lax.axis_size("sess"), lax.axis_size("tp")
    rows, dl = frames.shape
    d_all, head_cols = w_qkv.shape[1:]
    slots, ctx = kv_cache.shape[1:3]
    sessions = frame_session.shape[0]
    heads = head_cols // HD
    cap = (slots + n - 1) // n
    msg = (heads * cap + 15) // 16 * 16
    tchunk = 1024 // slots
    chunks = (ctx + tchunk - 1) // tchunk
    held, total, stack = heads * slots, n * msg, heads * rows
    parts = (ctx + 4 * tchunk - 1) // (4 * tchunk)
    dims = (n, tp, heads, cap, msg, rows, slots, ctx, tchunk, chunks)
    vmem = pl.BlockSpec(memory_space=pltpu.VMEM)
    hbm = pl.BlockSpec(memory_space=pl.ANY)
    dma = pltpu.SemaphoreType.DMA
    return pl.pallas_call(
        functools.partial(kernel, dims),
        out_shape=pltpu.VMEM((rows, dl), BF16),
        in_specs=[hbm] * 8,
        out_specs=vmem,
        scratch_shapes=[
            pltpu.VMEM((d_all // LANES, LANES), BF16),
            pltpu.VMEM((1, sessions), jnp.int32),
            pltpu.VMEM((1, sessions), jnp.int32),
            pltpu.VMEM((1, sessions), jnp.int32),
            pltpu.VMEM((3, d_all, head_cols), BF16),
            pltpu.VMEM((head_cols, d_all), BF16),
            pltpu.VMEM((2, chunks * tchunk, slots, head_cols), BF16),
            pltpu.VMEM((tp, rows, dl), BF16),
            pltpu.VMEM((rows, d_all), BF16),
            pltpu.VMEM((n, msg, HD), BF16),
            pltpu.VMEM((n, msg, HD), BF16),
            pltpu.VMEM((n, 2, msg, HD), BF16),
            pltpu.VMEM((n, 2, msg, HD), BF16),
            pltpu.VMEM((n, msg, HD), BF16),
            pltpu.VMEM((n, msg, HD), BF16),
            pltpu.VMEM((tp - 1, rows, dl), BF16),
            pltpu.VMEM((tp - 1, rows, dl), BF16),
            pltpu.VMEM((chunks, held, tchunk * slots), F32),
            pltpu.VMEM((held, head_cols), F32),
            pltpu.VMEM((total, stack), BF16),
            pltpu.VMEM((stack, total), BF16),
            pltpu.VMEM((held, total), BF16),
            pltpu.VMEM((total, held), BF16),
            pltpu.VMEM((held, LANES), F32),
            dma((5 + 3 + 2 * parts + 1,)),
            dma((tp - 1,)), dma((tp - 1,)),
            dma((n - 1,)), dma((n - 1,)),
            dma((n - 1,)), dma((n - 1,)),
            dma((n - 1,)), dma((n - 1,)),
            dma((tp - 1,)), dma((tp - 1,)),
        ],
        compiler_params=pltpu.CompilerParams(
            collective_id=0, has_side_effects=True, vmem_limit_bytes=60 * 1024 * 1024
        ),
        name="attention_step",
    )(
        frames,
        norm_gain.reshape(d_all // LANES, LANES),
        frame_session.reshape(1, sessions),
        owner_of.reshape(1, sessions),
        context_len.reshape(1, sessions),
        w_qkv,
        w_out,
        jnp.transpose(kv_cache, (0, 2, 1, 3)),
    )


def solution(mesh):
    in_specs = (
        P("sess", "tp"),
        P(),
        P(None, None, "tp"),
        P("tp", None),
        P(None, "sess", None, "tp"),
        P(),
        P(),
        P(),
    )
    out_specs = P("sess", "tp")
    return jax.shard_map(body, mesh=mesh, in_specs=in_specs, out_specs=out_specs, check_vma=False)
```

```python
import functools

import jax
import jax.numpy as jnp
from jax import lax
from jax.experimental import pallas as pl
from jax.experimental.pallas import tpu as pltpu
from jax.sharding import PartitionSpec as P

HD = 128
LANES = 128
MESH = pl.DeviceIdType.MESH
F32 = jnp.float32
BF16 = jnp.bfloat16


def quot(x, k):
    if k & (k - 1) == 0:
        return lax.shift_right_logical(x, jnp.full_like(x, k.bit_length() - 1))
    return lax.div(x, jnp.full_like(x, k))


def rest(x, k):
    return x - quot(x, k) * k


def iota(rows, cols, axis):
    return lax.broadcasted_iota(jnp.int32, (rows, cols), axis)


def one_hot(cond):
    return jnp.where(cond, 1.0, 0.0).astype(BF16)


def routing(me, n, heads, cap, msg, rows, slots, sessions, fs, owner, length):
    def pick(cond, values, axis):
        return jnp.sum(jnp.where(cond, values, 0.0), axis=axis, keepdims=True)

    i0, i1 = iota(sessions, sessions, 0), iota(sessions, sessions, 1)
    eye = i0 == i1

    def as_col(row):
        return pick(eye, row, 1)

    owner_c = as_col(owner)
    slot_c = pick((owner_c == owner) & (i1 < i0), 1.0, 1)
    match = i0 == fs
    row_owner = pick(match, owner_c, 0)
    row_slot = pick(match, slot_c, 0)
    row_len = pick(match, as_col(length), 0)
    row_owner_c, row_slot_c = as_col(row_owner), as_col(row_slot)
    block0, block1 = quot(i0, rows), quot(i1, rows)
    row_pair = pick((row_owner_c == row_owner) & (block0 == block1) & (i0 < i1), 1.0, 0)
    target = row_owner * cap + row_pair
    place = quot(iota(1, sessions, 1), rows).astype(F32) * cap + row_pair
    target_c, place_c = as_col(target), as_col(place)
    me_f = me.astype(F32)

    stack, total, held = heads * rows, n * msg, heads * slots

    def message_code(i):
        inner = rest(i, msg)
        return quot(inner, cap), (quot(i, msg) * cap + rest(inner, cap)).astype(F32)

    local = pick(
        iota(sessions, stack, 0) == me * rows + rest(iota(sessions, stack, 1), rows), target_c, 0
    )
    head_i, code = message_code(iota(total, stack, 0))
    send = one_hot((head_i == quot(iota(total, stack, 1), rows)) & (code == local))
    local_c = pick(
        iota(stack, sessions, 1) == me * rows + rest(iota(stack, sessions, 0), rows), target, 1
    )
    head_i, code = message_code(iota(stack, total, 1))
    unsend = one_hot((head_i == quot(iota(stack, total, 0), rows)) & (code == local_c))

    in_slot = (row_slot == rest(iota(held, sessions, 0), slots).astype(F32)) & (row_owner == me_f)
    _, code = message_code(iota(sessions, total, 1))
    spread = jnp.dot(one_hot(in_slot), one_hot(place_c == code), preferred_element_type=F32)
    head_i, _ = message_code(iota(held, total, 1))
    collect = jnp.where(head_i == quot(iota(held, total, 0), slots), spread, 0.0).astype(BF16)
    in_slot_t = (row_slot_c == rest(iota(sessions, held, 1), slots).astype(F32)) & (
        row_owner_c == me_f
    )
    _, code = message_code(iota(total, sessions, 0))
    spread = jnp.dot(one_hot(place == code), one_hot(in_slot_t), preferred_element_type=F32)
    head_i, _ = message_code(iota(total, held, 0))
    uncollect = jnp.where(head_i == quot(iota(total, held, 1), slots), spread, 0.0).astype(BF16)

    held_len = pick(in_slot, row_len, 1)
    lane = iota(held, LANES, 1)
    limit = jnp.where(
        rest(lane, slots) == rest(iota(held, LANES, 0), slots),
        held_len - quot(lane, slots).astype(F32),
        -1.0,
    )
    return send, unsend, collect, uncollect, limit


def kernel(
    dims,
    frames_hbm, gain_hbm, fs_hbm, owner_hbm, length_hbm, wqkv_hbm, wout_hbm, kv_hbm,
    out_ref,
    gain_v, fs_v, owner_v, length_v, w_v, wo_v, kv_v, fr_all, normed, q_send, q_recv, kv_send, kv_recv, r_send, r_recv,
    p_send, p_recv, scores, acc, send_m, unsend_m, collect_m, uncollect_m, limit_m,
    load_sem, ag_s, ag_r, q_s, q_r, kv_s, kv_r, r_s, r_r, p_s, p_r,
):
    n, tp, heads, cap, msg, rows, slots, ctx, tchunk, chunks = dims
    dl = frames_hbm.shape[1]
    d_all = dl * tp
    me, mt = lax.axis_index("sess"), lax.axis_index("tp")
    sess_peer = [lax.rem(me + d, n) for d in range(n)]
    tp_peer = [lax.rem(mt + d, tp) for d in range(tp)]

    loads = []

    def load(src, dst):
        loads.append(pltpu.make_async_copy(src, dst, load_sem.at[len(loads)]))
        loads[-1].start()
        return loads[-1]

    barrier = pltpu.get_barrier_semaphore()
    for d in range(1, tp):
        pl.semaphore_signal(barrier, inc=1, device_id=(me, tp_peer[d]), device_id_type=MESH)
    for d in range(1, n):
        pl.semaphore_signal(barrier, inc=1, device_id=(sess_peer[d], mt), device_id_type=MESH)
    small = [
        load(fs_hbm, fs_v),
        load(owner_hbm, owner_v),
        load(length_hbm, length_v),
        load(gain_hbm, gain_v),
        load(frames_hbm, fr_all.at[mt]),
    ]
    w_load = [load(wqkv_hbm.at[0], w_v.at[0])]
    pl.semaphore_wait(barrier, n + tp - 2)

    def over_tp(src, dst, s, r, d):
        copy = pltpu.make_async_remote_copy(
            src_ref=src, dst_ref=dst, send_sem=s.at[d - 1], recv_sem=r.at[d - 1],
            device_id=(me, tp_peer[d]), device_id_type=MESH,
        )
        copy.start()
        return copy

    def over_sess(send, recv, s, r):
        copies = []
        for d in range(1, n):
            copy = pltpu.make_async_remote_copy(
                src_ref=send.at[sess_peer[d]], dst_ref=recv.at[me],
                send_sem=s.at[d - 1], recv_sem=r.at[d - 1],
                device_id=(sess_peer[d], mt), device_id_type=MESH,
            )
            copy.start()
            copies.append(copy)
        return copies

    ag = [over_tp(frames_hbm, fr_all.at[mt], ag_s, ag_r, d) for d in range(1, tp)]
    w_load += [load(wqkv_hbm.at[c], w_v.at[c]) for c in (1, 2)]

    def load_cache(c):
        parts = []
        for t0 in range(0, ctx, 4 * tchunk):
            span = pl.ds(t0, min(4 * tchunk, ctx - t0))
            parts.append(load(kv_hbm.at[c, span], kv_v.at[c, span]))
        return parts

    key_load = load_cache(0)
    pad = chunks * tchunk - ctx
    if pad:
        kv_v[:, ctx:] = jnp.zeros((2, pad) + kv_v.shape[2:], BF16)
    for copy in small:
        copy.wait()
    send_m[...], unsend_m[...], collect_m[...], uncollect_m[...], limit_m[...] = routing(
        me, n, heads, cap, msg, rows, slots, fs_v.shape[1],
        fs_v[...], owner_v[...].astype(F32), length_v[...].astype(F32),
    )

    for copy in ag:
        copy.wait()
    square = jnp.zeros((rows, 1), F32)
    for b in range(tp):
        wide = fr_all[b].astype(F32)
        square += jnp.sum(wide * wide, axis=1, keepdims=True)
    scale = lax.rsqrt(square * (1.0 / d_all) + 1e-05)
    gain = gain_v[...].astype(F32)
    for b in range(tp):
        for t in range(dl // LANES):
            col = b * dl + t * LANES
            part = fr_all[b, :, t * LANES : (t + 1) * LANES].astype(F32) * scale
            part = part * gain[col // LANES : col // LANES + 1]
            normed[:, col : col + LANES] = part.astype(BF16)

    def project(c):
        w_load[c].wait()

        out = jnp.dot(normed[...], w_v[c], preferred_element_type=F32).astype(BF16)
        stacked = jnp.concatenate([out[:, h * HD : (h + 1) * HD] for h in range(heads)], axis=0)
        placed = jnp.dot(send_m[...], stacked, preferred_element_type=F32)
        return placed.astype(BF16).reshape(n, msg, HD)

    q_send[...] = project(0)
    q_copies = over_sess(q_send, q_recv, q_s, q_r)
    value_load = load_cache(1)
    q_recv[me] = q_send[me]
    kv_send[:, 0] = project(1)
    kv_send[:, 1] = project(2)
    kv_copies = over_sess(kv_send, kv_recv, kv_s, kv_r)
    wo_load = load(wout_hbm, wo_v)
    kv_recv[me] = kv_send[me]

    def collected(block):
        return jnp.dot(
            collect_m[...], block.reshape(n * msg, HD), preferred_element_type=F32
        )

    factor = 1.0 / jnp.sqrt(jnp.float32(HD))
    held = heads * slots
    for copy in q_copies:
        copy.wait()
    query = collected(q_recv[...])
    query_t = query.T
    head_lane = quot(iota(HD, held, 1), slots)
    query_wide = jnp.concatenate(
        [jnp.where(head_lane == h, query_t, 0.0) for h in range(heads)], axis=0
    ).astype(BF16)
    width = tchunk * slots
    tiles = width // LANES
    tile_t = LANES // slots
    limit = limit_m[...]

    def score_step(c, top):
        keys = kv_v[0, pl.ds(c * tchunk, tchunk)].reshape(width, heads * HD)
        s = jnp.dot(keys, query_wide, preferred_element_type=F32)
        for k in range(tiles):
            edge = float(c * tchunk + k * tile_t)
            tile = jnp.where(
                limit > edge, s[k * LANES : (k + 1) * LANES].T * factor, -jnp.inf
            )
            scores[c, :, k * LANES : (k + 1) * LANES] = tile
            top = jnp.maximum(top, tile)
        return top

    top = jnp.full((held, LANES), -jnp.inf, F32)
    for i, copy in enumerate(key_load):
        copy.wait()
        for c in range(4 * i, min(4 * i + 4, chunks)):
            top = score_step(c, top)

    for copy in kv_copies:
        copy.wait()
    new_key = collected(kv_recv[:, 0])
    new_value = collected(kv_recv[:, 1])
    own = jnp.sum(query * new_key, axis=1, keepdims=True) * factor
    top = jnp.maximum(jnp.max(top, axis=1, keepdims=True), own)
    top_wide = jnp.broadcast_to(top, (held, LANES))

    total = jnp.zeros((held, LANES), F32)
    for i, copy in enumerate(value_load):
        weights = []
        for c in range(4 * i, min(4 * i + 4, chunks)):
            for k in range(tiles):
                e = jnp.exp(scores[c, :, k * LANES : (k + 1) * LANES] - top_wide)
                total = total + e
                weights.append(e.astype(BF16))
        copy.wait()
        span = len(weights) * LANES
        values = kv_v[1, pl.ds(4 * i * tchunk, span // slots)].reshape(span, heads * HD)
        part = jnp.dot(jnp.concatenate(weights, axis=1), values, preferred_element_type=F32)
        acc[...] = part if i == 0 else acc[...] + part
    own_exp = jnp.exp(own - top)
    inverse = 1.0 / (jnp.sum(total, axis=1, keepdims=True) + own_exp)
    own_weight = own_exp.astype(BF16).astype(F32)
    mixed = jnp.concatenate(
        [acc[h * slots : (h + 1) * slots, h * HD : (h + 1) * HD] for h in range(heads)], axis=0
    )
    attended = ((mixed + own_weight * new_value) * inverse).astype(BF16)
    r_send[...] = (
        jnp.dot(uncollect_m[...], attended, preferred_element_type=F32)
        .astype(BF16)
        .reshape(n, msg, HD)
    )
    r_copies = over_sess(r_send, r_recv, r_s, r_r)
    r_recv[me] = r_send[me]
    wo_load.wait()
    for copy in r_copies:
        copy.wait()
    back = jnp.dot(
        unsend_m[...], r_recv[...].reshape(n * msg, HD), preferred_element_type=F32
    ).astype(BF16)
    mine = jnp.concatenate([back[h * rows : (h + 1) * rows] for h in range(heads)], axis=1)

    def branch(dest):
        block = wo_v[:, pl.ds(pl.multiple_of(dest * dl, dl), dl)]
        return jnp.dot(mine, block, preferred_element_type=F32)

    p_copies = []
    for d in range(1, tp):
        p_send[d - 1] = branch(tp_peer[d]).astype(BF16)
        p_copies.append(over_tp(p_send.at[d - 1], p_recv.at[d - 1], p_s, p_r, d))
    result = branch(mt)
    for d in range(1, tp):
        p_copies[d - 1].wait()
        result = result + p_recv[d - 1].astype(F32)
    out_ref[...] = (fr_all[mt].astype(F32) + result).astype(BF16)


def body(frames, norm_gain, w_qkv, w_out, kv_cache, frame_session, owner_of, context_len):
    n, tp = lax.axis_size("sess"), lax.axis_size("tp")
    rows, dl = frames.shape
    d_all, head_cols = w_qkv.shape[1:]
    slots, ctx = kv_cache.shape[1:3]
    sessions = frame_session.shape[0]
    heads = head_cols // HD
    cap = (slots + n - 1) // n
    msg = (heads * cap + 15) // 16 * 16
    tchunk = 1024 // slots
    chunks = (ctx + tchunk - 1) // tchunk
    held, total, stack = heads * slots, n * msg, heads * rows
    parts = (ctx + 4 * tchunk - 1) // (4 * tchunk)
    dims = (n, tp, heads, cap, msg, rows, slots, ctx, tchunk, chunks)
    vmem = pl.BlockSpec(memory_space=pltpu.VMEM)
    hbm = pl.BlockSpec(memory_space=pl.ANY)
    dma = pltpu.SemaphoreType.DMA
    return pl.pallas_call(
        functools.partial(kernel, dims),
        out_shape=pltpu.VMEM((rows, dl), BF16),
        in_specs=[hbm] * 8,
        out_specs=vmem,
        scratch_shapes=[
            pltpu.VMEM((d_all // LANES, LANES), BF16),
            pltpu.VMEM((1, sessions), jnp.int32),
            pltpu.VMEM((1, sessions), jnp.int32),
            pltpu.VMEM((1, sessions), jnp.int32),
            pltpu.VMEM((3, d_all, head_cols), BF16),
            pltpu.VMEM((head_cols, d_all), BF16),
            pltpu.VMEM((2, chunks * tchunk, slots, head_cols), BF16),
            pltpu.VMEM((tp, rows, dl), BF16),
            pltpu.VMEM((rows, d_all), BF16),
            pltpu.VMEM((n, msg, HD), BF16),
            pltpu.VMEM((n, msg, HD), BF16),
            pltpu.VMEM((n, 2, msg, HD), BF16),
            pltpu.VMEM((n, 2, msg, HD), BF16),
            pltpu.VMEM((n, msg, HD), BF16),
            pltpu.VMEM((n, msg, HD), BF16),
            pltpu.VMEM((tp - 1, rows, dl), BF16),
            pltpu.VMEM((tp - 1, rows, dl), BF16),
            pltpu.VMEM((chunks, held, tchunk * slots), F32),
            pltpu.VMEM((held, head_cols), F32),
            pltpu.VMEM((total, stack), BF16),
            pltpu.VMEM((stack, total), BF16),
            pltpu.VMEM((held, total), BF16),
            pltpu.VMEM((total, held), BF16),
            pltpu.VMEM((held, LANES), F32),
            dma((5 + 3 + 2 * parts + 1,)),
            dma((tp - 1,)), dma((tp - 1,)),
            dma((n - 1,)), dma((n - 1,)),
            dma((n - 1,)), dma((n - 1,)),
            dma((n - 1,)), dma((n - 1,)),
            dma((tp - 1,)), dma((tp - 1,)),
        ],
        compiler_params=pltpu.CompilerParams(
            collective_id=0, has_side_effects=True, vmem_limit_bytes=60 * 1024 * 1024
        ),
        name="attention_step",
    )(
        frames,
        norm_gain.reshape(d_all // LANES, LANES),
        frame_session.reshape(1, sessions),
        owner_of.reshape(1, sessions),
        context_len.reshape(1, sessions),
        w_qkv,
        w_out,
        jnp.transpose(kv_cache, (0, 2, 1, 3)),
    )


def solution(mesh):
    in_specs = (
        P("sess", "tp"),
        P(),
        P(None, None, "tp"),
        P("tp", None),
        P(None, "sess", None, "tp"),
        P(),
        P(),
        P(),
    )
    out_specs = P("sess", "tp")
    return jax.shard_map(body, mesh=mesh, in_specs=in_specs, out_specs=out_specs, check_vma=False)
```

```python
import functools

import jax
import jax.numpy as jnp
from jax import lax
from jax.experimental import pallas as pl
from jax.experimental.pallas import tpu as pltpu
from jax.sharding import PartitionSpec as P

HD = 128
LANES = 128
MESH = pl.DeviceIdType.MESH
F32 = jnp.float32
BF16 = jnp.bfloat16


def quot(x, k):
    if k & (k - 1) == 0:
        return lax.shift_right_logical(x, jnp.full_like(x, k.bit_length() - 1))
    return lax.div(x, jnp.full_like(x, k))


def rest(x, k):
    return x - quot(x, k) * k


def iota(rows, cols, axis):
    return lax.broadcasted_iota(jnp.int32, (rows, cols), axis)


def one_hot(cond):
    return jnp.where(cond, 1.0, 0.0).astype(BF16)


def routing(me, n, heads, cap, msg, rows, slots, sessions, fs, owner, length):
    def pick(cond, values, axis):
        return jnp.sum(jnp.where(cond, values, 0.0), axis=axis, keepdims=True)

    i0, i1 = iota(sessions, sessions, 0), iota(sessions, sessions, 1)
    eye = i0 == i1

    def as_col(row):
        return pick(eye, row, 1)

    owner_c = as_col(owner)
    slot_c = pick((owner_c == owner) & (i1 < i0), 1.0, 1)
    match = i0 == fs
    row_owner = pick(match, owner_c, 0)
    row_slot = pick(match, slot_c, 0)
    row_len = pick(match, as_col(length), 0)
    row_owner_c, row_slot_c = as_col(row_owner), as_col(row_slot)
    block0, block1 = quot(i0, rows), quot(i1, rows)
    row_pair = pick((row_owner_c == row_owner) & (block0 == block1) & (i0 < i1), 1.0, 0)
    target = row_owner * cap + row_pair
    place = quot(iota(1, sessions, 1), rows).astype(F32) * cap + row_pair
    target_c, place_c = as_col(target), as_col(place)
    me_f = me.astype(F32)

    stack, total, held = heads * rows, n * msg, heads * slots

    def message_code(i):
        inner = rest(i, msg)
        return quot(inner, cap), (quot(i, msg) * cap + rest(inner, cap)).astype(F32)

    local = pick(
        iota(sessions, stack, 0) == me * rows + rest(iota(sessions, stack, 1), rows), target_c, 0
    )
    head_i, code = message_code(iota(total, stack, 0))
    send = one_hot((head_i == quot(iota(total, stack, 1), rows)) & (code == local))
    in_slot = (row_slot == rest(iota(held, sessions, 0), slots).astype(F32)) & (row_owner == me_f)
    _, code = message_code(iota(sessions, total, 1))
    spread = jnp.dot(one_hot(in_slot), one_hot(place_c == code), preferred_element_type=F32)
    head_i, _ = message_code(iota(held, total, 1))
    collect = jnp.where(head_i == quot(iota(held, total, 0), slots), spread, 0.0).astype(BF16)
    in_slot_t = (row_slot_c == rest(iota(sessions, held, 1), slots).astype(F32)) & (
        row_owner_c == me_f
    )
    _, code = message_code(iota(total, sessions, 0))
    spread = jnp.dot(one_hot(place == code), one_hot(in_slot_t), preferred_element_type=F32)
    head_i, _ = message_code(iota(total, held, 0))
    uncollect = jnp.where(head_i == quot(iota(total, held, 1), slots), spread, 0.0).astype(BF16)

    held_len = pick(in_slot, row_len, 1)
    lane = iota(held, LANES, 1)
    limit = jnp.where(
        rest(lane, slots) == rest(iota(held, LANES, 0), slots),
        held_len - quot(lane, slots).astype(F32),
        -1.0,
    )
    return send, local, collect, uncollect, limit


def kernel(
    dims,
    frames_hbm, gain_hbm, fs_hbm, owner_hbm, length_hbm, wqkv_hbm, wout_hbm, kv_hbm,
    out_ref,
    gain_v, fs_v, owner_v, length_v, w_v, wo_v, kv_v, fr_all, normed, q_send, q_recv, kv_send, kv_recv, r_send, r_recv,
    p_send, p_recv, scores, acc, send_m, collect_m, uncollect_m, limit_m,
    load_sem, ag_s, ag_r, q_s, q_r, kv_s, kv_r, r_s, r_r, p_s, p_r,
):
    n, tp, heads, cap, msg, rows, slots, ctx, tchunk, chunks = dims
    dl = frames_hbm.shape[1]
    d_all = dl * tp
    me, mt = lax.axis_index("sess"), lax.axis_index("tp")
    sess_peer = [lax.rem(me + d, n) for d in range(n)]
    tp_peer = [lax.rem(mt + d, tp) for d in range(tp)]

    loads = []

    def load(src, dst):
        loads.append(pltpu.make_async_copy(src, dst, load_sem.at[len(loads)]))
        loads[-1].start()
        return loads[-1]

    barrier = pltpu.get_barrier_semaphore()
    for d in range(1, tp):
        pl.semaphore_signal(barrier, inc=1, device_id=(me, tp_peer[d]), device_id_type=MESH)
    for d in range(1, n):
        pl.semaphore_signal(barrier, inc=1, device_id=(sess_peer[d], mt), device_id_type=MESH)
    small = [
        load(fs_hbm, fs_v),
        load(owner_hbm, owner_v),
        load(length_hbm, length_v),
        load(gain_hbm, gain_v),
        load(frames_hbm, fr_all.at[mt]),
    ]
    w_load = [load(wqkv_hbm.at[0], w_v.at[0])]
    w_load += [load(wqkv_hbm.at[c], w_v.at[c]) for c in (1, 2)]

    def load_cache(c):
        parts = []
        for t0 in range(0, ctx, 2 * tchunk):
            span = pl.ds(t0, min(2 * tchunk, ctx - t0))
            parts.append(load(kv_hbm.at[c, span], kv_v.at[c, span]))
        return parts

    key_load = load_cache(0)
    value_load = load_cache(1)
    wo_load = load(wout_hbm, wo_v)
    pl.semaphore_wait(barrier, n + tp - 2)

    def over_tp(src, dst, s, r, d):
        copy = pltpu.make_async_remote_copy(
            src_ref=src, dst_ref=dst, send_sem=s.at[d - 1], recv_sem=r.at[d - 1],
            device_id=(me, tp_peer[d]), device_id_type=MESH,
        )
        copy.start()
        return copy

    def over_sess(send, recv, s, r):
        copies = []
        for d in range(1, n):
            copy = pltpu.make_async_remote_copy(
                src_ref=send.at[sess_peer[d]], dst_ref=recv.at[me],
                send_sem=s.at[d - 1], recv_sem=r.at[d - 1],
                device_id=(sess_peer[d], mt), device_id_type=MESH,
            )
            copy.start()
            copies.append(copy)
        return copies

    ag = [over_tp(frames_hbm, fr_all.at[mt], ag_s, ag_r, d) for d in range(1, tp)]
    pad = chunks * tchunk - ctx
    if pad:
        kv_v[:, ctx:] = jnp.zeros((2, pad) + kv_v.shape[2:], BF16)
    for copy in small:
        copy.wait()
    send_m[...], local, collect_m[...], uncollect_m[...], limit_m[...] = routing(
        me, n, heads, cap, msg, rows, slots, fs_v.shape[1],
        fs_v[...], owner_v[...].astype(F32), length_v[...].astype(F32),
    )

    for copy in ag:
        copy.wait()
    square = jnp.zeros((rows, 1), F32)
    for b in range(tp):
        wide = fr_all[b].astype(F32)
        square += jnp.sum(wide * wide, axis=1, keepdims=True)
    scale = lax.rsqrt(square * (1.0 / d_all) + 1e-05)
    gain = gain_v[...].astype(F32)
    for b in range(tp):
        for t in range(dl // LANES):
            col = b * dl + t * LANES
            part = fr_all[b, :, t * LANES : (t + 1) * LANES].astype(F32) * scale
            part = part * gain[col // LANES : col // LANES + 1]
            normed[:, col : col + LANES] = part.astype(BF16)

    def project(c):
        w_load[c].wait()

        out = jnp.dot(normed[...], w_v[c], preferred_element_type=F32).astype(BF16)
        stacked = jnp.concatenate([out[:, h * HD : (h + 1) * HD] for h in range(heads)], axis=0)
        placed = jnp.dot(send_m[...], stacked, preferred_element_type=F32)
        return placed.astype(BF16).reshape(n, msg, HD)

    q_send[...] = project(0)
    q_copies = over_sess(q_send, q_recv, q_s, q_r)
    q_recv[me] = q_send[me]
    kv_send[:, 0] = project(1)
    kv_send[:, 1] = project(2)
    kv_copies = over_sess(kv_send, kv_recv, kv_s, kv_r)
    kv_recv[me] = kv_send[me]

    def collected(block):
        return jnp.dot(
            collect_m[...], block.reshape(n * msg, HD), preferred_element_type=F32
        )

    factor = 1.0 / jnp.sqrt(jnp.float32(HD))
    held = heads * slots
    for copy in q_copies:
        copy.wait()
    query = collected(q_recv[...])
    query_t = query.T
    head_lane = quot(iota(HD, held, 1), slots)
    query_wide = jnp.concatenate(
        [jnp.where(head_lane == h, query_t, 0.0) for h in range(heads)], axis=0
    ).astype(BF16)
    width = tchunk * slots
    tiles = width // LANES
    tile_t = LANES // slots
    limit = limit_m[...]

    def score_step(c, top):
        keys = kv_v[0, pl.ds(c * tchunk, tchunk)].reshape(width, heads * HD)
        s = jnp.dot(keys, query_wide, preferred_element_type=F32)
        for k in range(tiles):
            edge = float(c * tchunk + k * tile_t)
            tile = jnp.where(
                limit > edge, s[k * LANES : (k + 1) * LANES].T * factor, -jnp.inf
            )
            scores[c, :, k * LANES : (k + 1) * LANES] = tile
            top = jnp.maximum(top, tile)
        return top

    top = jnp.full((held, LANES), -jnp.inf, F32)
    for i, copy in enumerate(key_load):
        copy.wait()
        for c in range(2 * i, min(2 * i + 2, chunks)):
            top = score_step(c, top)

    for copy in kv_copies:
        copy.wait()
    new_key = collected(kv_recv[:, 0])
    new_value = collected(kv_recv[:, 1])
    own = jnp.sum(query * new_key, axis=1, keepdims=True) * factor
    top = jnp.maximum(jnp.max(top, axis=1, keepdims=True), own)
    top_wide = jnp.broadcast_to(top, (held, LANES))

    total = jnp.zeros((held, LANES), F32)
    for i, copy in enumerate(value_load):
        weights = []
        for c in range(2 * i, min(2 * i + 2, chunks)):
            for k in range(tiles):
                e = jnp.exp(scores[c, :, k * LANES : (k + 1) * LANES] - top_wide)
                total = total + e
                weights.append(e.astype(BF16))
        copy.wait()
        span = len(weights) * LANES
        values = kv_v[1, pl.ds(2 * i * tchunk, span // slots)].reshape(span, heads * HD)
        part = jnp.dot(jnp.concatenate(weights, axis=1), values, preferred_element_type=F32)
        acc[...] = part if i == 0 else acc[...] + part
    own_exp = jnp.exp(own - top)
    inverse = 1.0 / (jnp.sum(total, axis=1, keepdims=True) + own_exp)
    own_weight = own_exp.astype(BF16).astype(F32)
    mixed = jnp.concatenate(
        [acc[h * slots : (h + 1) * slots, h * HD : (h + 1) * HD] for h in range(heads)], axis=0
    )
    attended = ((mixed + own_weight * new_value) * inverse).astype(BF16)
    r_send[...] = (
        jnp.dot(uncollect_m[...], attended, preferred_element_type=F32)
        .astype(BF16)
        .reshape(n, msg, HD)
    )
    r_copies = over_sess(r_send, r_recv, r_s, r_r)
    r_recv[me] = r_send[me]
    stack, count = heads * rows, n * msg
    eye = iota(stack, stack, 0) == iota(stack, stack, 1)
    local_c = jnp.sum(jnp.where(eye, local, 0.0), axis=1, keepdims=True)
    at = iota(stack, count, 1)
    inner = rest(at, msg)
    code = (quot(at, msg) * cap + rest(inner, cap)).astype(F32)
    same_head = quot(inner, cap) == quot(iota(stack, count, 0), rows)
    unsend = one_hot(same_head & (code == local_c))
    wo_load.wait()
    for copy in r_copies:
        copy.wait()
    back = jnp.dot(
        unsend, r_recv[...].reshape(n * msg, HD), preferred_element_type=F32
    ).astype(BF16)
    mine = jnp.concatenate([back[h * rows : (h + 1) * rows] for h in range(heads)], axis=1)

    def branch(dest):
        block = wo_v[:, pl.ds(pl.multiple_of(dest * dl, dl), dl)]
        return jnp.dot(mine, block, preferred_element_type=F32)

    p_copies = []
    for d in range(1, tp):
        p_send[d - 1] = branch(tp_peer[d]).astype(BF16)
        p_copies.append(over_tp(p_send.at[d - 1], p_recv.at[d - 1], p_s, p_r, d))
    result = branch(mt)
    for d in range(1, tp):
        p_copies[d - 1].wait()
        result = result + p_recv[d - 1].astype(F32)
    out_ref[...] = (fr_all[mt].astype(F32) + result).astype(BF16)


def body(frames, norm_gain, w_qkv, w_out, kv_cache, frame_session, owner_of, context_len):
    n, tp = lax.axis_size("sess"), lax.axis_size("tp")
    rows, dl = frames.shape
    d_all, head_cols = w_qkv.shape[1:]
    slots, ctx = kv_cache.shape[1:3]
    sessions = frame_session.shape[0]
    heads = head_cols // HD
    cap = (slots + n - 1) // n
    msg = (heads * cap + 15) // 16 * 16
    tchunk = 1024 // slots
    chunks = (ctx + tchunk - 1) // tchunk
    held, total, stack = heads * slots, n * msg, heads * rows
    parts = (ctx + 2 * tchunk - 1) // (2 * tchunk)
    dims = (n, tp, heads, cap, msg, rows, slots, ctx, tchunk, chunks)
    vmem = pl.BlockSpec(memory_space=pltpu.VMEM)
    hbm = pl.BlockSpec(memory_space=pl.ANY)
    dma = pltpu.SemaphoreType.DMA
    return pl.pallas_call(
        functools.partial(kernel, dims),
        out_shape=pltpu.VMEM((rows, dl), BF16),
        in_specs=[hbm] * 8,
        out_specs=vmem,
        scratch_shapes=[
            pltpu.VMEM((d_all // LANES, LANES), BF16),
            pltpu.VMEM((1, sessions), jnp.int32),
            pltpu.VMEM((1, sessions), jnp.int32),
            pltpu.VMEM((1, sessions), jnp.int32),
            pltpu.VMEM((3, d_all, head_cols), BF16),
            pltpu.VMEM((head_cols, d_all), BF16),
            pltpu.VMEM((2, chunks * tchunk, slots, head_cols), BF16),
            pltpu.VMEM((tp, rows, dl), BF16),
            pltpu.VMEM((rows, d_all), BF16),
            pltpu.VMEM((n, msg, HD), BF16),
            pltpu.VMEM((n, msg, HD), BF16),
            pltpu.VMEM((n, 2, msg, HD), BF16),
            pltpu.VMEM((n, 2, msg, HD), BF16),
            pltpu.VMEM((n, msg, HD), BF16),
            pltpu.VMEM((n, msg, HD), BF16),
            pltpu.VMEM((tp - 1, rows, dl), BF16),
            pltpu.VMEM((tp - 1, rows, dl), BF16),
            pltpu.VMEM((chunks, held, tchunk * slots), F32),
            pltpu.VMEM((held, head_cols), F32),
            pltpu.VMEM((total, stack), BF16),
            pltpu.VMEM((held, total), BF16),
            pltpu.VMEM((total, held), BF16),
            pltpu.VMEM((held, LANES), F32),
            dma((5 + 3 + 2 * parts + 1,)),
            dma((tp - 1,)), dma((tp - 1,)),
            dma((n - 1,)), dma((n - 1,)),
            dma((n - 1,)), dma((n - 1,)),
            dma((n - 1,)), dma((n - 1,)),
            dma((tp - 1,)), dma((tp - 1,)),
        ],
        compiler_params=pltpu.CompilerParams(
            collective_id=0, has_side_effects=True, vmem_limit_bytes=60 * 1024 * 1024
        ),
        name="attention_step",
    )(
        frames,
        norm_gain.reshape(d_all // LANES, LANES),
        frame_session.reshape(1, sessions),
        owner_of.reshape(1, sessions),
        context_len.reshape(1, sessions),
        w_qkv,
        w_out,
        jnp.transpose(kv_cache, (0, 2, 1, 3)),
    )


def solution(mesh):
    in_specs = (
        P("sess", "tp"),
        P(),
        P(None, None, "tp"),
        P("tp", None),
        P(None, "sess", None, "tp"),
        P(),
        P(),
        P(),
    )
    out_specs = P("sess", "tp")
    return jax.shard_map(body, mesh=mesh, in_specs=in_specs, out_specs=out_specs, check_vma=False)
```
